256 devices in a mesh: dp: 8 (over y, core), seq: 32 (over x, z).
Axes of the slice: x: 4, y: 4, z: 8, core: 2. Of those that a mesh axis runs over, the one named last changes fastest.
Arguments:
- spatial_query: bfloat16 [8, 32, 256, 1536], P('dp', 'seq'), may hold values from -6 to 6
- spatial_key: bfloat16 [8, 32, 256, 1536], P('dp', 'seq'), may hold values from -6 to 6
- spatial_value: bfloat16 [8, 32, 256, 1536], P('dp', 'seq'), may hold values from -6 to 6
- temporal_query: bfloat16 [8, 32, 256, 1536], P('dp', 'seq'), may hold values from -6 to 6
- temporal_key: bfloat16 [8, 32, 256, 1536], P('dp', 'seq'), may hold values from -6 to 6
- out_grad: bfloat16 [8, 32, 256, 1536], P('dp', 'seq'), may hold values from -6 to 6
- segment_ids: int32 [8, 32], P('dp'), may hold values from 0 to 3, never falling along the last dimension, each value on 1 to 16 neighbouring positions
- live_counts: int32 [8, 4], P('dp'), may hold values from 64 to 192, as said below
- norm_gains: float32 [4, 128], replicated, may hold values from 0.5 to 2
Outputs:
- block_out: bfloat16 [8, 32, 256, 1536], P('dp', 'seq')
- grad_spatial_query: bfloat16 [8, 32, 256, 1536], P('dp', 'seq')
- grad_spatial_key: bfloat16 [8, 32, 256, 1536], P('dp', 'seq')
- grad_spatial_value: bfloat16 [8, 32, 256, 1536], P('dp', 'seq')
- grad_temporal_query: bfloat16 [8, 32, 256, 1536], P('dp', 'seq')
- grad_temporal_key: bfloat16 [8, 32, 256, 1536], P('dp', 'seq')
- grad_gains: float32 [4, 128], replicated
The draws below stay inside these ranges and needn't reach their ends.
Inputs may be any that keep to these rules, and one draw needn't show every extreme that they name: `segment_ids`: segment numbers never fall along a buffer's frames; each sample holds 1 to 16 frames, and one sample of each buffer holds exactly that many. `live_counts`: every buffer has a sample with exactly 192 live positions.
All inputs are finite; a program needn't handle non-finite values.
Results may differ from the reference program's by a relative error of at most 0.03.
Values may be sent and summed in bfloat16 or wider, within the bound.
No kernel may reach another device: no remote copies, remote signals or barrier semaphores. Data moves between devices by JAX's collectives and lax.ppermute only.
A program may use at most 128 MiB of HBM per device.

```python
import math
import jax
import jax.numpy as jnp
import numpy as np
from jax import lax

HD = 128
FEAT = 1536
P_SIZE = 256
NSEG = 4
FRAMES = 32
GROUPS = 8


def draw_live_counts(key, part):
    key = jax.random.fold_in(key, 11)
    key_counts, key_pick = jax.random.split(key)
    most = P_SIZE - P_SIZE // 4
    counts = jax.random.randint(key_counts, (GROUPS, NSEG), P_SIZE // 4, most + 1, dtype=jnp.int32)
    picked = jax.random.randint(key_pick, (GROUPS, 1), 0, NSEG, dtype=jnp.int32)
    full = jnp.arange(NSEG, dtype=jnp.int32)[None, :] == picked
    return jnp.where(full, jnp.int32(most), counts).astype(jnp.int32)


def shard_levels(own_key, shape, shards, smallest, largest):
    level = 1.0
    for axis_at, blocks in shards:
        heights = jax.random.uniform(jax.random.fold_in(jax.random.fold_in(own_key, 6), axis_at), (blocks,), jnp.float32, smallest / len(shards), largest / len(shards))
        level = level * jnp.repeat(jnp.exp(heights), shape[axis_at] // blocks).reshape((-1,) + (1,) * (len(shape) - 1 - axis_at))
    return level


def profile(count, total, most, skew):
    loads = [(1 << 20) // math.isqrt(standing ** skew) + 1 for standing in range(2, count + 1)]
    rest, holding = total - most - (count - 1), [1] * (count - 1)
    while rest > 0:
        free = [i for i in range(count - 1) if holding[i] < most]
        whole, remaining = sum([loads[i] for i in free]), rest
        for i in free:
            more = min(most - holding[i], max(1, remaining * loads[i] // whole), rest)
            holding[i] = holding[i] + more
            rest = rest - more
    return np.array([most] + holding)


def ragged_sizes(stream_key, count, total, bound, slope):
    if count == 2:
        one = jax.random.randint(stream_key, (), max(1, total - bound), min(bound, total - 1) + 1)
        return jnp.stack([one, total - one])
    tallies = jnp.asarray(profile(count, total, bound, slope), jnp.int32)
    pairs = (count - 1) // 2
    source_of, receiver = tallies[1:1 + 2 * pairs:2], tallies[2:2 + 2 * pairs:2]
    margin = jnp.minimum(source_of - 1, bound - receiver)
    shifted = jax.random.randint(jax.random.fold_in(stream_key, 1), (pairs,), 0, 1 << 20) % (margin + 1)
    tallies = tallies.at[1:1 + 2 * pairs:2].set(source_of - shifted).at[2:2 + 2 * pairs:2].set(receiver + shifted)
    return tallies[jax.random.permutation(jax.random.fold_in(stream_key, 2), count)]


def noise(stream_key, shape, deviation, bound, shards=(), kind=jnp.bfloat16):
    level = shard_levels(stream_key, shape, shards, -0.22, 0.18) if shards else 1.0
    entries = jax.random.normal(stream_key, shape, jnp.float32) * deviation * level
    return jnp.minimum(jnp.maximum(entries, -bound), bound).astype(kind)


def setup_inputs(seed: int = 0) -> dict:
    streams_of = jax.random.split(jax.random.key(seed), 10)
    spatial_query = noise(streams_of[0], (GROUPS, FRAMES, P_SIZE, FEAT), 1.0, 6.0, ((0, 8), (1, 32)))
    spatial_key = noise(streams_of[1], (GROUPS, FRAMES, P_SIZE, FEAT), 1.0, 6.0, ((0, 8), (1, 32)))
    spatial_value = noise(streams_of[2], (GROUPS, FRAMES, P_SIZE, FEAT), 1.0, 6.0, ((0, 8), (1, 32)))
    temporal_query = noise(streams_of[3], (GROUPS, FRAMES, P_SIZE, FEAT), 1.0, 6.0, ((0, 8), (1, 32)))
    temporal_key = noise(streams_of[4], (GROUPS, FRAMES, P_SIZE, FEAT), 1.0, 6.0, ((0, 8), (1, 32)))
    out_grad = noise(streams_of[5], (GROUPS, FRAMES, P_SIZE, FEAT), 1.0, 6.0, ((0, 8), (1, 32)))
    segment_ids = jax.vmap(lambda own: jnp.searchsorted(jnp.cumsum(ragged_sizes(own, NSEG, FRAMES, FRAMES // 2, 1)), jnp.arange(FRAMES), side="right"))(jax.random.split(streams_of[6], GROUPS)).reshape((GROUPS, FRAMES)).astype(jnp.int32)
    live_counts = draw_live_counts(jax.random.fold_in(streams_of[9], 71), 0)
    norm_gains = jnp.clip(jnp.exp(jax.random.uniform(streams_of[8], (4, HD), jnp.float32, math.log(0.5), math.log(2.0))), 0.5, 2.0)
    return dict(spatial_query=spatial_query, spatial_key=spatial_key, spatial_value=spatial_value, temporal_query=temporal_query, temporal_key=temporal_key, out_grad=out_grad, segment_ids=segment_ids, live_counts=live_counts, norm_gains=norm_gains)


def rms_scale(values, gain):
    wide = values.astype(jnp.float32)
    factor = lax.rsqrt(lax.optimization_barrier(jnp.mean(wide * wide, axis=-1, keepdims=True)) + 1e-06)
    return (wide * factor * gain).astype(jnp.bfloat16)

def frame_counts(segment, counts):
    onehot = segment[:, None] == jnp.arange(counts.shape[0], dtype=jnp.int32)[None, :]
    return lax.optimization_barrier(jnp.sum(jnp.where(onehot, counts[None, :], 0), axis=1)).astype(jnp.int32)

def spatial_attention(query, keys_in, value, gain_q, gain_k, key_live):
    frame_count, pos_count, width = query.shape
    head_size = gain_q.shape[0]
    head_count = width // head_size
    shape4 = (frame_count, pos_count, head_count, head_size)
    normed_q = rms_scale(query.reshape(shape4), gain_q)
    normed_k = rms_scale(keys_in.reshape(shape4), gain_k)
    scores = jnp.einsum('fphd,fqhd->fhpq', normed_q, normed_k, preferred_element_type=jnp.float32) * head_size ** (-0.5)
    scores = jnp.where(key_live[:, None, None, :], scores, -1e+30)
    weights = jax.nn.softmax(scores, axis=-1).astype(jnp.bfloat16)
    result = jnp.einsum('fhpq,fqhd->fphd', weights, value.reshape(shape4), preferred_element_type=jnp.float32)
    return result.astype(jnp.bfloat16).reshape(frame_count, pos_count, width)

def temporal_attention(query, keys_in, value, gain_q, gain_k, segment, counts_frame, pos_start):
    frame_count, pos_count, width = query.shape
    head_size = gain_q.shape[0]
    head_count = width // head_size
    shape4 = (frame_count, pos_count, head_count, head_size)
    normed_q = rms_scale(query.reshape(shape4), gain_q)
    normed_k = rms_scale(keys_in.reshape(shape4), gain_k)
    scores = jnp.einsum('fphd,gphd->phfg', normed_q, normed_k, preferred_element_type=jnp.float32) * head_size ** (-0.5)
    same_sample = segment[:, None] == segment[None, :]
    scores = jnp.where(same_sample[None, None, :, :], scores, -1e+30)
    weights = jax.nn.softmax(scores, axis=-1).astype(jnp.bfloat16)
    result = jnp.einsum('phfg,gphd->fphd', weights, value.reshape(shape4), preferred_element_type=jnp.float32)
    places = pos_start + jnp.arange(pos_count, dtype=jnp.int32)
    live_here = (places[None, :] < counts_frame[:, None]).astype(jnp.float32)
    return result.reshape(frame_count, pos_count, width) * live_here[:, :, None]

def reference(spatial_query, spatial_key, spatial_value, temporal_query, temporal_key, out_grad, segment_ids, live_counts, norm_gains):

    def one_buffer(inputs):
        s_query, s_key, s_value, t_query, t_key, cotangent, segment, counts = inputs
        counts_frame = frame_counts(segment, counts)
        key_live = jnp.arange(s_query.shape[1], dtype=jnp.int32)[None, :] < counts_frame[:, None]

        def spatial_part(query, keys_in, value, gain_q, gain_k):
            return spatial_attention(query, keys_in, value, gain_q, gain_k, key_live)

        def temporal_part(query, keys_in, value, gain_q, gain_k):
            return temporal_attention(query, keys_in, value, gain_q, gain_k, segment, counts_frame, jnp.int32(0))
        spatial_out, back_spatial = jax.vjp(spatial_part, s_query, s_key, s_value, norm_gains[0], norm_gains[1])
        temporal_out, back_temporal = jax.vjp(temporal_part, t_query, t_key, spatial_out, norm_gains[2], norm_gains[3])
        result = temporal_out.astype(jnp.bfloat16)
        grad_tq, grad_tk, grad_sout, gain_tq, gain_tk = back_temporal(cotangent.astype(jnp.float32))
        grad_sq, grad_sk, grad_sv, gain_sq, gain_sk = back_spatial(grad_sout)
        return (result, grad_sq, grad_sk, grad_sv, grad_tq, grad_tk, jnp.stack([gain_sq, gain_sk, gain_tq, gain_tk]))
    outputs = lax.map(one_buffer, (spatial_query, spatial_key, spatial_value, temporal_query, temporal_key, out_grad, segment_ids, live_counts))
    return (outputs[0], outputs[1], outputs[2], outputs[3], outputs[4], outputs[5], lax.optimization_barrier(jnp.sum(outputs[6], axis=0)))
```

```python
import math

import jax
import jax.numpy as jnp
from jax import lax
from jax.experimental import pallas as pl
from jax.experimental.pallas import tpu as pltpu
from jax.sharding import PartitionSpec as P

HD = 128
POS = 256
LIVE = 192
FEAT = 1536
SEQ = 32
DP = 8
XS = 4
ZS = 8
ROWS = LIVE // ZS
COLS = FEAT // XS
HEADS = COLS // HD
EPS = 1e-6
SCALE = HD ** -0.5
SCALE2 = SCALE * math.log2(math.e)
BF = jnp.bfloat16
F32 = jnp.float32


def dot_nt(a, b):
    return lax.dot_general(a, b, (((1,), (1,)), ((), ())), preferred_element_type=F32)


def dot_nn(a, b):
    return lax.dot_general(a, b, (((1,), (0,)), ((), ())), preferred_element_type=F32)


def dot_tn(a, b):
    return lax.dot_general(a, b, (((0,), (0,)), ((), ())), preferred_element_type=F32)


def unit(x):
    factor = lax.rsqrt(jnp.mean(x * x, axis=-1, keepdims=True) + EPS)
    return x * factor, factor


def unit_back(grad, hat, factor, gain):
    gd = grad * gain
    dx = factor * (gd - hat * jnp.mean(gd * hat, axis=-1, keepdims=True))
    return dx, jnp.sum(grad * hat, axis=0, keepdims=True)


def count_of(me_ref, seg_ref, counts_ref):
    return counts_ref[0, seg_ref[0, me_ref[0]]]


def prep_kernel(me_ref, seg_ref, counts_ref, tq_ref, tk_ref, og_ref, out_ref):
    count = count_of(me_ref, seg_ref, counts_ref)
    out_ref[:, 0] = tq_ref[0, 0].reshape(ZS, ROWS, COLS)
    out_ref[:, 1] = tk_ref[0, 0].reshape(ZS, ROWS, COLS)
    rows = lax.broadcasted_iota(jnp.int32, (LIVE, COLS), 0)
    og = jnp.where(rows < count, og_ref[0, 0].astype(F32), 0.0)
    out_ref[:, 2] = og.reshape(ZS, ROWS, COLS).astype(BF)


def spatial_weights(nq, nk, live_keys):
    e = jnp.exp2(dot_nt(nk, nq) * SCALE2)
    e = jnp.where(live_keys, e, 0.0)
    return e * (1.0 / jnp.sum(e, axis=0, keepdims=True))


def spatial_fwd_kernel(me_ref, seg_ref, counts_ref, gains_ref, q_ref, k_ref, v_ref, out_ref):
    count = count_of(me_ref, seg_ref, counts_ref)
    live_keys = lax.broadcasted_iota(jnp.int32, (LIVE, LIVE), 0) < count
    live_rows = lax.broadcasted_iota(jnp.int32, (LIVE, HD), 0) < count
    for h in range(HEADS):
        at = slice(h * HD, (h + 1) * HD)
        qh, _ = unit(q_ref[0, 0, :, at].astype(F32))
        kh, _ = unit(k_ref[0, 0, :, at].astype(F32))
        nq = (qh * gains_ref[0:1, :]).astype(BF)
        nk = (kh * gains_ref[1:2, :]).astype(BF)
        w = spatial_weights(nq, nk, live_keys)
        so = dot_tn(w.astype(BF), v_ref[0, 0, :, at])
        so = jnp.where(live_rows, so, 0.0)
        out_ref[:, :, at] = so.reshape(ZS, ROWS, HD).astype(BF)


def spatial_bwd_kernel(
    me_ref, seg_ref, counts_ref, gains_ref, q_ref, k_ref, v_ref, g_ref, dq_ref, dk_ref, dv_ref, gg_ref
):
    @pl.when(pl.program_id(0) == 0)
    def _():
        gg_ref[...] = jnp.zeros_like(gg_ref)

    count = count_of(me_ref, seg_ref, counts_ref)
    live_keys = lax.broadcasted_iota(jnp.int32, (LIVE, LIVE), 0) < count
    for ref in (dq_ref, dk_ref, dv_ref):
        ref[0, 0, LIVE:, :] = jnp.zeros((POS - LIVE, COLS), BF)
    for h in range(HEADS):
        at = slice(h * HD, (h + 1) * HD)
        gq, gk = gains_ref[0:1, :], gains_ref[1:2, :]
        qh, qf = unit(q_ref[0, 0, :, at].astype(F32))
        kh, kf = unit(k_ref[0, 0, :, at].astype(F32))
        nq = (qh * gq).astype(BF)
        nk = (kh * gk).astype(BF)
        v = v_ref[0, 0, :, at]
        g = g_ref[:, :, at].astype(F32).reshape(LIVE, HD).astype(BF)
        w = spatial_weights(nq, nk, live_keys)
        dv = dot_nn(w.astype(BF), g)
        dw = dot_nt(v, g).astype(BF).astype(F32)
        ds = w * (dw - jnp.sum(dw * w, axis=0, keepdims=True))
        ds = (ds * SCALE).astype(BF)
        dnq = dot_tn(ds, nk).astype(BF).astype(F32)
        dnk = dot_nn(ds, nq).astype(BF).astype(F32)
        dq, sq = unit_back(dnq, qh, qf, gq)
        dk, sk = unit_back(dnk, kh, kf, gk)
        dq_ref[0, 0, :LIVE, at] = dq.astype(BF)
        dk_ref[0, 0, :LIVE, at] = dk.astype(BF)
        dv_ref[0, 0, :LIVE, at] = dv.astype(BF)
        gg_ref[0:1, :] += sq
        gg_ref[1:2, :] += sk


def temporal_kernel(
    gains_ref, mask_ref, tq_ref, tk_ref, og_ref, so_ref, dso_ref, back_ref, gg_ref
):
    @pl.when(pl.program_id(0) == 0)
    def _():
        gg_ref[...] = jnp.zeros_like(gg_ref)

    gq, gk = gains_ref[2:3, :], gains_ref[3:4, :]
    mask = mask_ref[...]
    tq = tq_ref[:, 0].astype(F32)
    tk = tk_ref[:, 0].astype(F32)
    og = og_ref[:, 0].astype(F32)
    so = so_ref[...].astype(F32)
    parts = []
    for j in range(ROWS // 8):
        def cut(a):
            return a[:, 8 * j : 8 * j + 8, :].reshape(SEQ * 8, HD)

        qh, qf = unit(cut(tq))
        kh, kf = unit(cut(tk))
        g = cut(og).astype(BF)
        v = cut(so).astype(BF)
        nq = (qh * gq).astype(BF)
        nk = (kh * gk).astype(BF)
        e = jnp.exp2(dot_nt(nk, nq) * SCALE2) * mask
        w = e * (1.0 / jnp.sum(e, axis=0, keepdims=True))
        wb = w.astype(BF)
        o = dot_tn(wb, v)
        dso = dot_nn(wb, g)
        dw = dot_nt(v, g).astype(BF).astype(F32)
        ds = w * (dw - jnp.sum(dw * w, axis=0, keepdims=True))
        ds = (ds * SCALE).astype(BF)
        dnq = dot_tn(ds, nk).astype(BF).astype(F32)
        dnk = dot_nn(ds, nq).astype(BF).astype(F32)
        dq, sq = unit_back(dnq, qh, qf, gq)
        dk, sk = unit_back(dnk, kh, kf, gk)
        gg_ref[0:1, :] += sq
        gg_ref[1:2, :] += sk
        parts.append([a.reshape(SEQ, 8, HD) for a in (dso, o, dq, dk)])
    dso, o, dq, dk = [jnp.concatenate(a, axis=1).astype(BF) for a in zip(*parts)]
    dso_ref[...] = dso
    back_ref[:, 0] = o
    back_ref[:, 1] = dq
    back_ref[:, 2] = dk


def finish_kernel(o_ref, dtq_ref, dtk_ref, o_out, dtq_out, dtk_out):
    for src, dst in ((o_ref, o_out), (dtq_ref, dtq_out), (dtk_ref, dtk_out)):
        dst[0, 0, LIVE:, :] = jnp.zeros((POS - LIVE, COLS), BF)
        dst[0, 0, :LIVE, :] = src[:, 0].astype(F32).reshape(LIVE, COLS).astype(BF)


SMEM = pl.BlockSpec(memory_space=pltpu.SMEM)
PARAMS = pltpu.CompilerParams(vmem_limit_bytes=48 << 20)


def cost(flops, arrays):
    return pl.CostEstimate(flops=flops, bytes_accessed=arrays * 2 * LIVE * FEAT, transcendentals=0)


def live_block():
    return pl.BlockSpec((1, 1, LIVE, COLS), lambda i: (0, 0, 0, i))


def full_block():
    return pl.BlockSpec((1, 1, POS, COLS), lambda i: (0, 0, 0, i))


def packed_block():
    return pl.BlockSpec((ZS, ROWS, COLS), lambda i: (i, 0, 0))


def reduce_all(values):
    for bit in (1, 2, 4):
        values = values + lax.ppermute(values, "dp", [(i, i ^ bit) for i in range(DP)])
    for bit in (1, 2, 4, 8, 16):
        values = values + lax.ppermute(values, "seq", [(i, i ^ bit) for i in range(SEQ)])
    return values


def per_device(sq, sk, sv, tq, tk, og, segment_ids, live_counts, norm_gains):
    me = lax.axis_index("seq").astype(jnp.int32).reshape(1)
    places = (me, segment_ids, live_counts)
    full = jax.ShapeDtypeStruct((1, 1, POS, FEAT), BF)
    packed = jax.ShapeDtypeStruct((SEQ, ROWS, COLS), BF)
    packed3 = jax.ShapeDtypeStruct((SEQ, 3, ROWS, COLS), BF)
    gains_spec = pl.BlockSpec((4, HD), lambda i: (0, 0))
    gg_spec = pl.BlockSpec((2, HD), lambda i: (0, 0))
    gg_shape = jax.ShapeDtypeStruct((2, HD), F32)

    sent = pl.pallas_call(
        prep_kernel,
        name="prep",
        grid=(XS,),
        out_shape=packed3,
        in_specs=[SMEM] * 3 + [live_block()] * 3,
        out_specs=pl.BlockSpec((ZS, 3, ROWS, COLS), lambda i: (i, 0, 0, 0)),
        compiler_params=PARAMS,
        cost_estimate=cost(0, 6),
    )(*places, tq, tk, og)
    got = lax.all_to_all(sent, "seq", split_axis=0, concat_axis=0, tiled=True)

    so = pl.pallas_call(
        spatial_fwd_kernel,
        name="spatial_fwd",
        grid=(XS,),
        out_shape=packed,
        in_specs=[SMEM] * 3 + [gains_spec] + [live_block()] * 3,
        out_specs=packed_block(),
        compiler_params=PARAMS,
        cost_estimate=cost(4 * LIVE * LIVE * FEAT, 4),
    )(*places, norm_gains, sq, sk, sv)
    so_pos = lax.all_to_all(so, "seq", split_axis=0, concat_axis=0, tiled=True)

    seg = jnp.repeat(segment_ids[0], 8)
    pos = jnp.arange(SEQ * 8, dtype=jnp.int32) % 8
    mask = (seg[:, None] == seg[None, :]) & (pos[:, None] == pos[None, :])
    mask = mask.astype(F32)

    def part(n):
        return pl.BlockSpec((SEQ, 1, ROWS, HD), lambda i: (0, n, 0, i))

    head_block = pl.BlockSpec((SEQ, ROWS, HD), lambda i: (0, 0, i))
    dso, back, gains_t = pl.pallas_call(
        temporal_kernel,
        name="temporal",
        grid=(HEADS,),
        out_shape=[packed, packed3, gg_shape],
        in_specs=[gains_spec, pl.BlockSpec((256, 256), lambda i: (0, 0)), part(0), part(1), part(2), head_block],
        out_specs=[head_block, pl.BlockSpec((SEQ, 3, ROWS, HD), lambda i: (0, 0, 0, i)), gg_spec],
        compiler_params=PARAMS,
        cost_estimate=cost(14 * 9 * 256 * 256 * HD, 8),
    )(norm_gains, mask, got, got, got, so_pos)

    dso_f = lax.all_to_all(dso, "seq", split_axis=0, concat_axis=0, tiled=True)
    back = lax.all_to_all(back, "seq", split_axis=0, concat_axis=0, tiled=True)

    dsq, dsk, dsv, gains_s = pl.pallas_call(
        spatial_bwd_kernel,
        name="spatial_bwd",
        grid=(XS,),
        out_shape=[full, full, full, gg_shape],
        in_specs=[SMEM] * 3 + [gains_spec] + [live_block()] * 3 + [packed_block()],
        out_specs=[full_block()] * 3 + [gg_spec],
        compiler_params=PARAMS,
        cost_estimate=cost(14 * LIVE * LIVE * FEAT, 8),
    )(*places, norm_gains, sq, sk, sv, dso_f)
    gains = reduce_all(jnp.concatenate([gains_s, gains_t], axis=0))

    def piece(n):
        return pl.BlockSpec((ZS, 1, ROWS, COLS), lambda i: (i, n, 0, 0))

    o, dtq, dtk = pl.pallas_call(
        finish_kernel,
        name="finish",
        grid=(XS,),
        out_shape=[full] * 3,
        in_specs=[piece(0), piece(1), piece(2)],
        out_specs=[full_block()] * 3,
        compiler_params=PARAMS,
        cost_estimate=cost(0, 6),
    )(back, back, back)
    return o, dsq, dsk, dsv, dtq, dtk, gains


def solution(mesh):
    big = P("dp", "seq", None, None)
    return jax.shard_map(
        per_device,
        mesh=mesh,
        in_specs=(big,) * 6 + (P("dp", None), P("dp", None), P()),
        out_specs=(big,) * 6 + (P(),),
        check_vma=False,
    )
```

```python
import math

import jax
import jax.numpy as jnp
from jax import lax
from jax.experimental import pallas as pl
from jax.experimental.pallas import tpu as pltpu
from jax.sharding import PartitionSpec as P

HD = 128
POS = 256
LIVE = 192
FEAT = 1536
SEQ = 32
DP = 8
XS = 4
ZS = 8
ROWS = LIVE // ZS
COLS = FEAT // XS
HEADS = COLS // HD
EPS = 1e-6
SCALE = HD ** -0.5
SCALE2 = SCALE * math.log2(math.e)
BF = jnp.bfloat16
F32 = jnp.float32


def dot_nt(a, b):
    return lax.dot_general(a, b, (((1,), (1,)), ((), ())), preferred_element_type=F32)


def dot_nn(a, b):
    return lax.dot_general(a, b, (((1,), (0,)), ((), ())), preferred_element_type=F32)


def dot_tn(a, b):
    return lax.dot_general(a, b, (((0,), (0,)), ((), ())), preferred_element_type=F32)


def unit(x):
    factor = lax.rsqrt(jnp.mean(x * x, axis=-1, keepdims=True) + EPS)
    return x * factor, factor


def unit_back(grad, hat, factor, gain):
    gd = grad * gain
    dx = factor * (gd - hat * jnp.mean(gd * hat, axis=-1, keepdims=True))
    return dx, jnp.sum(grad * hat, axis=0, keepdims=True)


def count_of(place_ref, seg_ref, counts_ref):
    return counts_ref[0, seg_ref[0, place_ref[0]]]


def prep_kernel(place_ref, seg_ref, counts_ref, tq_ref, tk_ref, og_ref, out_ref):
    count = count_of(place_ref, seg_ref, counts_ref)
    out_ref[:, 0] = tq_ref[0, 0].astype(F32).reshape(ZS, ROWS, COLS).astype(BF)
    out_ref[:, 1] = tk_ref[0, 0].astype(F32).reshape(ZS, ROWS, COLS).astype(BF)
    rows = lax.broadcasted_iota(jnp.int32, (LIVE, COLS), 0)
    og = jnp.where(rows < count, og_ref[0, 0].astype(F32), 0.0)
    out_ref[:, 2] = og.reshape(ZS, ROWS, COLS).astype(BF)


def spatial_weights(nq, nk, live_keys):
    e = jnp.exp2(dot_nt(nk, nq) * SCALE2)
    e = jnp.where(live_keys, e, 0.0)
    return e * (1.0 / jnp.sum(e, axis=0, keepdims=True))


def spatial_fwd_kernel(place_ref, seg_ref, counts_ref, gains_ref, q_ref, k_ref, v_ref, out_ref):
    count = count_of(place_ref, seg_ref, counts_ref)
    live_keys = lax.broadcasted_iota(jnp.int32, (LIVE, LIVE), 0) < count
    live_rows = lax.broadcasted_iota(jnp.int32, (LIVE, HD), 0) < count
    for h in range(HEADS):
        at = slice(h * HD, (h + 1) * HD)
        qh, _ = unit(q_ref[0, 0, :, at].astype(F32))
        kh, _ = unit(k_ref[0, 0, :, at].astype(F32))
        nq = (qh * gains_ref[0:1, :]).astype(BF)
        nk = (kh * gains_ref[1:2, :]).astype(BF)
        w = spatial_weights(nq, nk, live_keys)
        so = dot_tn(w.astype(BF), v_ref[0, 0, :, at])
        so = jnp.where(live_rows, so, 0.0)
        out_ref[:, :, at] = so.reshape(ZS, ROWS, HD).astype(BF)


def spatial_bwd_kernel(
    place_ref, seg_ref, counts_ref, gains_ref, q_ref, k_ref, v_ref, g_ref, dq_ref, dk_ref, dv_ref, gg_ref
):
    @pl.when(pl.program_id(0) == 0)
    def _():
        gg_ref[...] = jnp.zeros_like(gg_ref)

    count = count_of(place_ref, seg_ref, counts_ref)
    live_keys = lax.broadcasted_iota(jnp.int32, (LIVE, LIVE), 0) < count
    for ref in (dq_ref, dk_ref, dv_ref):
        ref[0, 0, LIVE:, :] = jnp.zeros((POS - LIVE, COLS), BF)
    for h in range(HEADS):
        at = slice(h * HD, (h + 1) * HD)
        gq, gk = gains_ref[0:1, :], gains_ref[1:2, :]
        qh, qf = unit(q_ref[0, 0, :, at].astype(F32))
        kh, kf = unit(k_ref[0, 0, :, at].astype(F32))
        nq = (qh * gq).astype(BF)
        nk = (kh * gk).astype(BF)
        v = v_ref[0, 0, :, at]
        g = g_ref[:, :, at].astype(F32).reshape(LIVE, HD).astype(BF)
        w = spatial_weights(nq, nk, live_keys)
        dv = dot_nn(w.astype(BF), g)
        dw = dot_nt(v, g).astype(BF).astype(F32)
        ds = w * (dw - jnp.sum(dw * w, axis=0, keepdims=True))
        ds = (ds * SCALE).astype(BF)
        dnq = dot_tn(ds, nk).astype(BF).astype(F32)
        dnk = dot_nn(ds, nq).astype(BF).astype(F32)
        dq, sq = unit_back(dnq, qh, qf, gq)
        dk, sk = unit_back(dnk, kh, kf, gk)
        dq_ref[0, 0, :LIVE, at] = dq.astype(BF)
        dk_ref[0, 0, :LIVE, at] = dk.astype(BF)
        dv_ref[0, 0, :LIVE, at] = dv.astype(BF)
        gg_ref[0:1, :] += sq
        gg_ref[1:2, :] += sk


def cut(a, j):
    return a[:, 8 * j : 8 * j + 8, :].reshape(SEQ * 8, HD)


def paste(parts):
    return jnp.concatenate([a.reshape(SEQ, 8, HD) for a in parts], axis=1).astype(BF)


def temporal_weights(qh, kh, gq, gk, mask):
    nq = (qh * gq).astype(BF)
    nk = (kh * gk).astype(BF)
    e = jnp.exp2(dot_nt(nk, nq) * SCALE2) * mask
    return nq, nk, e * (1.0 / jnp.sum(e, axis=0, keepdims=True))


def temporal_value_kernel(gains_ref, mask_ref, tq_ref, tk_ref, og_ref, dso_ref):
    gq, gk = gains_ref[2:3, :], gains_ref[3:4, :]
    mask = mask_ref[...]
    tq, tk, og = [ref[:, 0].astype(F32) for ref in (tq_ref, tk_ref, og_ref)]
    parts = []
    for j in range(ROWS // 8):
        qh, _ = unit(cut(tq, j))
        kh, _ = unit(cut(tk, j))
        _, _, w = temporal_weights(qh, kh, gq, gk, mask)
        parts.append(dot_nn(w.astype(BF), cut(og, j).astype(BF)))
    dso_ref[...] = paste(parts)


def temporal_kernel(gains_ref, mask_ref, tq_ref, tk_ref, og_ref, so_ref, two_ref, one_ref, gg_ref):
    @pl.when(pl.program_id(0) == 0)
    def _():
        gg_ref[...] = jnp.zeros_like(gg_ref)

    gq, gk = gains_ref[2:3, :], gains_ref[3:4, :]
    mask = mask_ref[...]
    tq, tk, og = [ref[:, 0].astype(F32) for ref in (tq_ref, tk_ref, og_ref)]
    so = so_ref[...].astype(F32)
    parts = []
    for j in range(ROWS // 8):
        qh, qf = unit(cut(tq, j))
        kh, kf = unit(cut(tk, j))
        g = cut(og, j).astype(BF)
        v = cut(so, j).astype(BF)
        nq, nk, w = temporal_weights(qh, kh, gq, gk, mask)
        o = dot_tn(w.astype(BF), v)
        dw = dot_nt(v, g).astype(BF).astype(F32)
        ds = w * (dw - jnp.sum(dw * w, axis=0, keepdims=True))
        ds = (ds * SCALE).astype(BF)
        dnq = dot_tn(ds, nk).astype(BF).astype(F32)
        dnk = dot_nn(ds, nq).astype(BF).astype(F32)
        dq, sq = unit_back(dnq, qh, qf, gq)
        dk, sk = unit_back(dnk, kh, kf, gk)
        gg_ref[0:1, :] += sq
        gg_ref[1:2, :] += sk
        parts.append([o, dq])
        one_ref[:, j] = dk.reshape(SEQ, 8, HD).astype(BF)
    for n, array in enumerate(zip(*parts)):
        two_ref[:, n] = paste(array)


def finish_two_kernel(o_ref, dtq_ref, o_out, dtq_out):
    for src, dst in ((o_ref, o_out), (dtq_ref, dtq_out)):
        dst[0, 0, LIVE:, :] = jnp.zeros((POS - LIVE, COLS), BF)
        dst[0, 0, :LIVE, :] = src[:, 0].astype(F32).reshape(LIVE, COLS).astype(BF)


def finish_one_kernel(src, dst):
    dst[0, 0, LIVE:, :] = jnp.zeros((POS - LIVE, COLS), BF)
    for h in range(HEADS):
        part = src[:, 3 * h : 3 * h + 3].astype(F32).reshape(LIVE, HD)
        dst[0, 0, :LIVE, h * HD : (h + 1) * HD] = part.astype(BF)


SMEM = pl.BlockSpec(memory_space=pltpu.SMEM)
PARAMS = pltpu.CompilerParams(vmem_limit_bytes=48 << 20)
WIDE = pltpu.CompilerParams(vmem_limit_bytes=60 << 20)


def cost(flops, arrays):
    return pl.CostEstimate(flops=flops, bytes_accessed=arrays * 2 * LIVE * FEAT, transcendentals=0)


def exchange(values):
    return lax.all_to_all(values, "seq", split_axis=0, concat_axis=0, tiled=True)


def reduce_dp(values):
    for bit in (1, 2, 4):
        values = values + lax.ppermute(values, "dp", [(i, i ^ bit) for i in range(DP)])
    return values


def split_wide(values):
    high = lax.reduce_precision(values, 8, 7)
    return jnp.concatenate([high, values - high], axis=0).astype(BF)


def live_block():
    return pl.BlockSpec((1, 1, LIVE, COLS), lambda i: (0, 0, 0, i))


def full_block():
    return pl.BlockSpec((1, 1, POS, COLS), lambda i: (0, 0, 0, i))


def packed_block():
    return pl.BlockSpec((ZS, ROWS, COLS), lambda i: (i, 0, 0))


def per_device(sq, sk, sv, tq, tk, og, segment_ids, live_counts, norm_gains):
    me = lax.axis_index("seq").astype(jnp.int32).reshape(1)
    places = (me, segment_ids, live_counts)
    full = jax.ShapeDtypeStruct((1, 1, POS, FEAT), BF)
    packed = jax.ShapeDtypeStruct((SEQ, ROWS, COLS), BF)
    packed2 = jax.ShapeDtypeStruct((SEQ, 2, ROWS, COLS), BF)
    packed3 = jax.ShapeDtypeStruct((SEQ, 3, ROWS, COLS), BF)
    tiles = jax.ShapeDtypeStruct((SEQ, 10, 8, HD), BF)
    gains_spec = pl.BlockSpec((4, HD), lambda i: (0, 0))
    gg_spec = pl.BlockSpec((2, HD), lambda i: (0, 0))
    gg_shape = jax.ShapeDtypeStruct((2, HD), F32)

    sent = pl.pallas_call(
        prep_kernel,
        name="prep",
        grid=(XS,),
        out_shape=packed3,
        in_specs=[SMEM] * 3 + [live_block()] * 3,
        out_specs=pl.BlockSpec((ZS, 3, ROWS, COLS), lambda i: (i, 0, 0, 0)),
        compiler_params=WIDE,
        cost_estimate=cost(0, 6),
    )(*places, tq, tk, og)
    got = exchange(sent)

    so = pl.pallas_call(
        spatial_fwd_kernel,
        name="spatial_fwd",
        grid=(XS,),
        out_shape=packed,
        in_specs=[SMEM] * 3 + [gains_spec] + [live_block()] * 3,
        out_specs=packed_block(),
        compiler_params=PARAMS,
        cost_estimate=cost(4 * LIVE * LIVE * FEAT, 4),
    )(*places, norm_gains, sq, sk, sv)
    seg = jnp.repeat(segment_ids[0], 8)
    pos = jnp.arange(SEQ * 8, dtype=jnp.int32) % 8
    mask = (seg[:, None] == seg[None, :]) & (pos[:, None] == pos[None, :])
    mask = mask.astype(F32)
    got, so, mask = lax.optimization_barrier((got, so, mask))
    so = exchange(so)

    def part(n):
        return pl.BlockSpec((SEQ, 1, ROWS, HD), lambda i: (0, n, 0, i))

    mask_spec = pl.BlockSpec((SEQ * 8, SEQ * 8), lambda i: (0, 0))
    head_block = pl.BlockSpec((SEQ, ROWS, HD), lambda i: (0, 0, i))
    dso = pl.pallas_call(
        temporal_value_kernel,
        name="temporal_value",
        grid=(HEADS,),
        out_shape=packed,
        in_specs=[gains_spec, mask_spec, part(0), part(1), part(2)],
        out_specs=head_block,
        compiler_params=WIDE,
        cost_estimate=cost(4 * 9 * 256 * 256 * HD, 4),
    )(norm_gains, mask, got, got, got)
    dso, so = lax.optimization_barrier((dso, so))
    dso = exchange(dso)

    two, one, gains_t = pl.pallas_call(
        temporal_kernel,
        name="temporal",
        grid=(HEADS,),
        out_shape=[packed2, tiles, gg_shape],
        in_specs=[gains_spec, mask_spec, part(0), part(1), part(2), head_block],
        out_specs=[
            pl.BlockSpec((SEQ, 2, ROWS, HD), lambda i: (0, 0, 0, i)),
            pl.BlockSpec((SEQ, 3, 8, HD), lambda i: (0, i, 0, 0)),
            gg_spec,
        ],
        compiler_params=WIDE,
        cost_estimate=cost(12 * 9 * 256 * 256 * HD, 7),
    )(norm_gains, mask, got, got, got, so)
    two, dso = lax.optimization_barrier((two, dso))
    two = exchange(two)

    dsq, dsk, dsv, gains_s = pl.pallas_call(
        spatial_bwd_kernel,
        name="spatial_bwd",
        grid=(XS,),
        out_shape=[full, full, full, gg_shape],
        in_specs=[SMEM] * 3 + [gains_spec] + [live_block()] * 3 + [packed_block()],
        out_specs=[full_block()] * 3 + [gg_spec],
        compiler_params=PARAMS,
        cost_estimate=cost(14 * LIVE * LIVE * FEAT, 8),
    )(*places, norm_gains, sq, sk, sv, dso)
    gains = split_wide(reduce_dp(jnp.concatenate([gains_s, gains_t], axis=0)))

    one = one.at[:, 9].set(jnp.broadcast_to(gains, (SEQ, 8, HD)))
    one, two = lax.optimization_barrier((one, two))
    one = exchange(one)
    gains = one[:, 9].astype(F32)
    gains = jnp.sum(gains[:, :4] + gains[:, 4:], axis=0)

    def piece(n):
        return pl.BlockSpec((ZS, 1, ROWS, COLS), lambda i: (i, n, 0, 0))

    o, dtq = pl.pallas_call(
        finish_two_kernel,
        name="finish_two",
        grid=(XS,),
        out_shape=[full] * 2,
        in_specs=[piece(0), piece(1)],
        out_specs=[full_block()] * 2,
        compiler_params=WIDE,
        cost_estimate=cost(0, 4),
    )(two, two)
    dtk = pl.pallas_call(
        finish_one_kernel,
        name="finish_one",
        grid=(XS,),
        out_shape=full,
        in_specs=[pl.BlockSpec((ZS, 10, 8, HD), lambda i: (i, 0, 0, 0))],
        out_specs=full_block(),
        compiler_params=WIDE,
        cost_estimate=cost(0, 2),
    )(one)
    return o, dsq, dsk, dsv, dtq, dtk, gains


def solution(mesh):
    big = P("dp", "seq", None, None)
    return jax.shard_map(
        per_device,
        mesh=mesh,
        in_specs=(big,) * 6 + (P("dp", None), P("dp", None), P()),
        out_specs=(big,) * 6 + (P(),),
        check_vma=False,
    )
```

```python
import math

import jax
import jax.numpy as jnp
from jax import lax
from jax.experimental import pallas as pl
from jax.experimental.pallas import tpu as pltpu
from jax.sharding import PartitionSpec as P

HD = 128
POS = 256
LIVE = 192
FEAT = 1536
SEQ = 32
DP = 8
XS = 4
ZS = 8
ROWS = LIVE // ZS
COLS = FEAT // XS
HEADS = COLS // HD
EPS = 1e-6
SCALE = HD ** -0.5
SCALE2 = SCALE * math.log2(math.e)
BF = jnp.bfloat16
F32 = jnp.float32


def dot_nt(a, b):
    return lax.dot_general(a, b, (((1,), (1,)), ((), ())), preferred_element_type=F32)


def dot_nn(a, b):
    return lax.dot_general(a, b, (((1,), (0,)), ((), ())), preferred_element_type=F32)


def dot_tn(a, b):
    return lax.dot_general(a, b, (((0,), (0,)), ((), ())), preferred_element_type=F32)


def unit(x):
    factor = lax.rsqrt(jnp.mean(x * x, axis=-1, keepdims=True) + EPS)
    return x * factor, factor


def unit_back(grad, hat, factor, gain):
    gd = grad * gain
    dx = factor * (gd - hat * jnp.mean(gd * hat, axis=-1, keepdims=True))
    return dx, jnp.sum(grad * hat, axis=0, keepdims=True)


def count_of(place_ref, seg_ref, counts_ref):
    return counts_ref[0, seg_ref[0, place_ref[0]]]


def spatial_weights(nq, nk, live_keys):
    e = jnp.exp2(dot_nt(nk, nq) * SCALE2)
    e = jnp.where(live_keys, e, 0.0)
    return e * (1.0 / jnp.sum(e, axis=0, keepdims=True))


def pack_kernel(
    me_ref, seg_ref, counts_ref, gains_ref, tq_ref, tk_ref, og_ref, q_ref, k_ref, v_ref, out_ref
):
    count = count_of(me_ref, seg_ref, counts_ref)
    live_keys = lax.broadcasted_iota(jnp.int32, (LIVE, LIVE), 0) < count
    live_rows = lax.broadcasted_iota(jnp.int32, (LIVE, HD), 0) < count

    def put(n, at, values):
        out_ref[:, n, :, at] = values.reshape(ZS, ROWS, HD).astype(BF)

    for h in range(HEADS):
        at = slice(h * HD, (h + 1) * HD)
        put(0, at, tq_ref[0, 0, :, at].astype(F32))
        put(1, at, tk_ref[0, 0, :, at].astype(F32))
        put(2, at, jnp.where(live_rows, og_ref[0, 0, :, at].astype(F32), 0.0))
        qh, _ = unit(q_ref[0, 0, :, at].astype(F32))
        kh, _ = unit(k_ref[0, 0, :, at].astype(F32))
        nq = (qh * gains_ref[0:1, :]).astype(BF)
        nk = (kh * gains_ref[1:2, :]).astype(BF)
        w = spatial_weights(nq, nk, live_keys)
        so = dot_tn(w.astype(BF), v_ref[0, 0, :, at])
        put(3, at, jnp.where(live_rows, so, 0.0))


def spatial_bwd_kernel(
    place_ref, seg_ref, counts_ref, gains_ref, q_ref, k_ref, v_ref, g_ref, dq_ref, dk_ref, dv_ref, gg_ref
):
    @pl.when(pl.program_id(0) == 0)
    def _():
        gg_ref[...] = jnp.zeros_like(gg_ref)

    count = count_of(place_ref, seg_ref, counts_ref)
    live_keys = lax.broadcasted_iota(jnp.int32, (LIVE, LIVE), 0) < count
    for ref in (dq_ref, dk_ref, dv_ref):
        ref[0, 0, LIVE:, :] = jnp.zeros((POS - LIVE, COLS), BF)
    for h in range(HEADS):
        at = slice(h * HD, (h + 1) * HD)
        gq, gk = gains_ref[0:1, :], gains_ref[1:2, :]
        qh, qf = unit(q_ref[0, 0, :, at].astype(F32))
        kh, kf = unit(k_ref[0, 0, :, at].astype(F32))
        nq = (qh * gq).astype(BF)
        nk = (kh * gk).astype(BF)
        v = v_ref[0, 0, :, at]
        g = g_ref[:, :, at].astype(F32).reshape(LIVE, HD).astype(BF)
        w = spatial_weights(nq, nk, live_keys)
        dv = dot_nn(w.astype(BF), g)
        dw = dot_nt(v, g).astype(BF).astype(F32)
        ds = w * (dw - jnp.sum(dw * w, axis=0, keepdims=True))
        ds = (ds * SCALE).astype(BF)
        dnq = dot_tn(ds, nk).astype(BF).astype(F32)
        dnk = dot_nn(ds, nq).astype(BF).astype(F32)
        dq, sq = unit_back(dnq, qh, qf, gq)
        dk, sk = unit_back(dnk, kh, kf, gk)
        dq_ref[0, 0, :LIVE, at] = dq.astype(BF)
        dk_ref[0, 0, :LIVE, at] = dk.astype(BF)
        dv_ref[0, 0, :LIVE, at] = dv.astype(BF)
        gg_ref[0:1, :] += sq
        gg_ref[1:2, :] += sk


def cut(a, j):
    return a[:, 8 * j : 8 * j + 8, :].reshape(SEQ * 8, HD)


def paste(parts):
    return jnp.concatenate([a.reshape(SEQ, 8, HD) for a in parts], axis=1).astype(BF)


def temporal_weights(qh, kh, gq, gk, mask):
    nq = (qh * gq).astype(BF)
    nk = (kh * gk).astype(BF)
    e = jnp.exp2(dot_nt(nk, nq) * SCALE2) * mask
    return nq, nk, e * (1.0 / jnp.sum(e, axis=0, keepdims=True))


def temporal_value_kernel(gains_ref, mask_ref, tq_ref, tk_ref, og_ref, out_ref):
    gq, gk = gains_ref[2:3, :], gains_ref[3:4, :]
    mask = mask_ref[...]
    tq, tk, og = [ref[:, 0].astype(F32) for ref in (tq_ref, tk_ref, og_ref)]
    parts = []
    for j in range(ROWS // 8):
        qh, _ = unit(cut(tq, j))
        kh, _ = unit(cut(tk, j))
        _, _, w = temporal_weights(qh, kh, gq, gk, mask)
        parts.append(dot_nn(w.astype(BF), cut(og, j).astype(BF)))
    out_ref[...] = paste(parts)


def temporal_kernel(gains_ref, mask_ref, tq_ref, tk_ref, og_ref, so_ref, out_ref, gg_ref):
    @pl.when(pl.program_id(0) == 0)
    def _():
        gg_ref[...] = jnp.zeros_like(gg_ref)

    gq, gk = gains_ref[2:3, :], gains_ref[3:4, :]
    mask = mask_ref[...]
    tq, tk, og, so = [ref[:, 0].astype(F32) for ref in (tq_ref, tk_ref, og_ref, so_ref)]
    parts = []
    for j in range(ROWS // 8):
        qh, qf = unit(cut(tq, j))
        kh, kf = unit(cut(tk, j))
        g = cut(og, j).astype(BF)
        v = cut(so, j).astype(BF)
        nq, nk, w = temporal_weights(qh, kh, gq, gk, mask)
        o = dot_tn(w.astype(BF), v)
        dw = dot_nt(v, g).astype(BF).astype(F32)
        ds = w * (dw - jnp.sum(dw * w, axis=0, keepdims=True))
        ds = (ds * SCALE).astype(BF)
        dnq = dot_tn(ds, nk).astype(BF).astype(F32)
        dnk = dot_nn(ds, nq).astype(BF).astype(F32)
        dq, sq = unit_back(dnq, qh, qf, gq)
        dk, sk = unit_back(dnk, kh, kf, gk)
        gg_ref[0:1, :] += sq
        gg_ref[1:2, :] += sk
        parts.append([o, dq, dk])
    for n, array in enumerate(zip(*parts)):
        out_ref[:, n] = paste(array)


def finish_kernel(*refs):
    n = len(refs) // 2
    for src, dst in zip(refs[:n], refs[n:]):
        dst[0, 0, LIVE:, :] = jnp.zeros((POS - LIVE, COLS), BF)
        dst[0, 0, :LIVE, :] = src[:, 0].astype(F32).reshape(LIVE, COLS).astype(BF)


SMEM = pl.BlockSpec(memory_space=pltpu.SMEM)
PARAMS = pltpu.CompilerParams(vmem_limit_bytes=48 << 20)
WIDE = pltpu.CompilerParams(vmem_limit_bytes=60 << 20)


def cost(flops, arrays):
    return pl.CostEstimate(flops=flops, bytes_accessed=arrays * 2 * LIVE * FEAT, transcendentals=0)


def exchange(values):
    return lax.all_to_all(values, "seq", split_axis=0, concat_axis=0, tiled=True)


def flips(values, axis, masks):
    size = lax.axis_size(axis)
    return [lax.ppermute(values, axis, [(i, i ^ mask) for i in range(size)]) for mask in masks]


def add_flips(values, axis, a, b):
    one, two, both = flips(values, axis, (a, b, a ^ b))
    return (values + one) + (two + both)


def live_block():
    return pl.BlockSpec((1, 1, LIVE, COLS), lambda i: (0, 0, 0, i))


def full_block():
    return pl.BlockSpec((1, 1, POS, COLS), lambda i: (0, 0, 0, i))


def piece(n):
    return pl.BlockSpec((ZS, 1, ROWS, COLS), lambda i: (i, n, 0, 0))


def finish(packed, places):
    full = jax.ShapeDtypeStruct((1, 1, POS, FEAT), BF)
    return pl.pallas_call(
        finish_kernel,
        name="finish",
        grid=(XS,),
        out_shape=[full] * len(places),
        in_specs=[piece(n) for n in places],
        out_specs=[full_block()] * len(places),
        compiler_params=WIDE,
        cost_estimate=cost(0, 2 * len(places)),
    )(*[packed] * len(places))


def per_device(sq, sk, sv, tq, tk, og, segment_ids, live_counts, norm_gains):
    me = lax.axis_index("seq").astype(jnp.int32).reshape(1)
    places = (me, segment_ids, live_counts)
    full = jax.ShapeDtypeStruct((1, 1, POS, FEAT), BF)
    packed = jax.ShapeDtypeStruct((SEQ, ROWS, COLS), BF)
    packed3 = jax.ShapeDtypeStruct((SEQ, 3, ROWS, COLS), BF)
    gains_spec = pl.BlockSpec((4, HD), lambda i: (0, 0))
    gg_spec = pl.BlockSpec((2, HD), lambda i: (0, 0))
    gg_shape = jax.ShapeDtypeStruct((2, HD), F32)

    sent = pl.pallas_call(
        pack_kernel,
        name="pack",
        grid=(XS,),
        out_shape=jax.ShapeDtypeStruct((SEQ, 4, ROWS, COLS), BF),
        in_specs=[SMEM] * 3 + [gains_spec] + [live_block()] * 6,
        out_specs=pl.BlockSpec((ZS, 4, ROWS, COLS), lambda i: (i, 0, 0, 0)),
        compiler_params=WIDE,
        cost_estimate=cost(4 * LIVE * LIVE * FEAT, 10),
    )(*places, norm_gains, tq, tk, og, sq, sk, sv)
    got = exchange(sent)

    seg = jnp.repeat(segment_ids[0], 8)
    pos = jnp.arange(SEQ * 8, dtype=jnp.int32) % 8
    mask = (seg[:, None] == seg[None, :]) & (pos[:, None] == pos[None, :])
    got, mask = lax.optimization_barrier((got, mask.astype(F32)))

    def part(n):
        return pl.BlockSpec((SEQ, 1, ROWS, HD), lambda i: (0, n, 0, i))

    temporal_in = [gains_spec, pl.BlockSpec((SEQ * 8, SEQ * 8), lambda i: (0, 0))]
    temporal_in += [part(n) for n in range(4)]
    dso = pl.pallas_call(
        temporal_value_kernel,
        name="temporal_value",
        grid=(HEADS,),
        out_shape=packed,
        in_specs=temporal_in[:-1],
        out_specs=pl.BlockSpec((SEQ, ROWS, HD), lambda i: (0, 0, i)),
        compiler_params=WIDE,
        cost_estimate=cost(4 * 9 * 256 * 256 * HD, 4),
    )(norm_gains, mask, got, got, got)
    got, dso = lax.optimization_barrier((got, dso))
    dso = exchange(dso)

    back, gains_t = pl.pallas_call(
        temporal_kernel,
        name="temporal",
        grid=(HEADS,),
        out_shape=[packed3, gg_shape],
        in_specs=temporal_in,
        out_specs=[pl.BlockSpec((SEQ, 3, ROWS, HD), lambda i: (0, 0, 0, i)), gg_spec],
        compiler_params=WIDE,
        cost_estimate=cost(12 * 9 * 256 * 256 * HD, 7),
    )(norm_gains, mask, got, got, got, got)
    back, dso = lax.optimization_barrier((back, dso))
    back = exchange(back)

    dsq, dsk, dsv, gains_s = pl.pallas_call(
        spatial_bwd_kernel,
        name="spatial_bwd",
        grid=(XS,),
        out_shape=[full, full, full, gg_shape],
        in_specs=[SMEM] * 3 + [gains_spec] + [live_block()] * 3 + [pl.BlockSpec((ZS, ROWS, COLS), lambda i: (i, 0, 0))],
        out_specs=[full_block()] * 3 + [gg_spec],
        compiler_params=PARAMS,
        cost_estimate=cost(14 * LIVE * LIVE * FEAT, 8),
    )(*places, norm_gains, sq, sk, sv, dso)
    gains = jnp.concatenate([gains_s, gains_t], axis=0)
    gains = gains + flips(gains, "dp", (1,))[0]
    gains = add_flips(gains, "dp", 2, 4)
    gains = add_flips(gains, "seq", 8, 16)
    gains = add_flips(gains, "seq", 1, 4)
    gains, back = lax.optimization_barrier((gains, back))
    gains = gains + flips(gains, "seq", (2,))[0]
    o, dtq, dtk = finish(back, [0, 1, 2])
    return o, dsq, dsk, dsv, dtq, dtk, gains


def solution(mesh):
    big = P("dp", "seq", None, None)
    return jax.shard_map(
        per_device,
        mesh=mesh,
        in_specs=(big,) * 6 + (P("dp", None), P("dp", None), P()),
        out_specs=(big,) * 6 + (P(),),
        check_vma=False,
    )
```

```python
import math

import jax
import jax.numpy as jnp
from jax import lax
from jax.experimental import pallas as pl
from jax.experimental.pallas import tpu as pltpu
from jax.sharding import PartitionSpec as P

HD = 128
POS = 256
LIVE = 192
FEAT = 1536
SEQ = 32
DP = 8
XS = 4
ZS = 8
ROWS = LIVE // ZS
COLS = FEAT // XS
HEADS = COLS // HD
PACK_XS = 2
EPS = 1e-6
SCALE = HD ** -0.5
SCALE2 = SCALE * math.log2(math.e)
BF = jnp.bfloat16
F32 = jnp.float32


def dot_nt(a, b):
    return lax.dot_general(a, b, (((1,), (1,)), ((), ())), preferred_element_type=F32)


def dot_nn(a, b):
    return lax.dot_general(a, b, (((1,), (0,)), ((), ())), preferred_element_type=F32)


def dot_tn(a, b):
    return lax.dot_general(a, b, (((0,), (0,)), ((), ())), preferred_element_type=F32)


def unit(x):
    factor = lax.rsqrt(jnp.mean(x * x, axis=-1, keepdims=True) + EPS)
    return x * factor, factor


def unit_back(grad, hat, factor, gain):
    gd = grad * gain
    dx = factor * (gd - hat * jnp.mean(gd * hat, axis=-1, keepdims=True))
    return dx, jnp.sum(grad * hat, axis=0, keepdims=True)


def count_of(place_ref, seg_ref, counts_ref):
    return counts_ref[0, seg_ref[0, place_ref[0]]]


def spatial_weights(nq, nk, live_keys):
    e = jnp.exp2(dot_nt(nk, nq) * SCALE2)
    e = jnp.where(live_keys, e, 0.0)
    return e * (1.0 / jnp.sum(e, axis=0, keepdims=True))


def pack_kernel(
    me_ref, seg_ref, counts_ref, gains_ref, tq_ref, tk_ref, og_ref, q_ref, k_ref, v_ref, out_ref
):
    count = count_of(me_ref, seg_ref, counts_ref)
    live_rows = lax.broadcasted_iota(jnp.int32, (LIVE, HD), 0) < count
    ones = jnp.where(live_rows, 1.0, 0.0).astype(BF)
    for h in range(HEADS * PACK_XS):
        at = slice(h * HD, (h + 1) * HD)
        x, to = h // HEADS, slice(h % HEADS * HD, (h % HEADS + 1) * HD)

        def put(n, values):
            out_ref[x * ZS : (x + 1) * ZS, n, :, to] = values.reshape(ZS, ROWS, HD).astype(BF)

        put(0, tq_ref[0, 0, :, at].astype(F32))
        put(1, tk_ref[0, 0, :, at].astype(F32))
        put(2, jnp.where(live_rows, og_ref[0, 0, :, at].astype(F32), 0.0))
        qh, _ = unit(q_ref[0, 0, :, at].astype(F32))
        kh, _ = unit(k_ref[0, 0, :, at].astype(F32))
        nq = (qh * gains_ref[0:1, :]).astype(BF)
        nk = (kh * gains_ref[1:2, :]).astype(BF)
        e = jnp.exp2(dot_nt(nq, nk) * SCALE2).astype(BF)
        v = jnp.where(live_rows, v_ref[0, 0, :, at].astype(F32), 0.0).astype(BF)
        both = dot_nn(e, jnp.concatenate([v, ones], axis=1))
        put(3, jnp.where(live_rows, both[:, :HD] * (1.0 / both[:, HD:]), 0.0))


def spatial_bwd_kernel(
    place_ref, seg_ref, counts_ref, gains_ref, q_ref, k_ref, v_ref, g_ref, dq_ref, dk_ref, dv_ref, gg_ref
):
    @pl.when(pl.program_id(0) == 0)
    def _():
        gg_ref[...] = jnp.zeros_like(gg_ref)

    count = count_of(place_ref, seg_ref, counts_ref)
    live_keys = lax.broadcasted_iota(jnp.int32, (LIVE, LIVE), 0) < count
    for ref in (dq_ref, dk_ref, dv_ref):
        ref[0, 0, LIVE:, :] = jnp.zeros((POS - LIVE, COLS), BF)
    for h in range(HEADS):
        at = slice(h * HD, (h + 1) * HD)
        gq, gk = gains_ref[0:1, :], gains_ref[1:2, :]
        qh, qf = unit(q_ref[0, 0, :, at].astype(F32))
        kh, kf = unit(k_ref[0, 0, :, at].astype(F32))
        nq = (qh * gq).astype(BF)
        nk = (kh * gk).astype(BF)
        v = v_ref[0, 0, :, at]
        g = g_ref[:, :, at].astype(F32).reshape(LIVE, HD).astype(BF)
        w = spatial_weights(nq, nk, live_keys)
        dv = dot_nn(w.astype(BF), g)
        dw = dot_nt(v, g).astype(BF).astype(F32)
        ds = w * (dw - jnp.sum(dw * w, axis=0, keepdims=True))
        ds = (ds * SCALE).astype(BF)
        dnq = dot_tn(ds, nk).astype(BF).astype(F32)
        dnk = dot_nn(ds, nq).astype(BF).astype(F32)
        dq, sq = unit_back(dnq, qh, qf, gq)
        dk, sk = unit_back(dnk, kh, kf, gk)
        dq_ref[0, 0, :LIVE, at] = dq.astype(BF)
        dk_ref[0, 0, :LIVE, at] = dk.astype(BF)
        dv_ref[0, 0, :LIVE, at] = dv.astype(BF)
        gg_ref[0:1, :] += sq
        gg_ref[1:2, :] += sk


def cut(a, j):
    return a[:, 8 * j : 8 * j + 8, :].reshape(SEQ * 8, HD)


def paste(parts):
    return jnp.concatenate([a.reshape(SEQ, 8, HD) for a in parts], axis=1).astype(BF)


def temporal_weights(qh, kh, gq, gk, mask):
    nq = (qh * gq).astype(BF)
    nk = (kh * gk).astype(BF)
    e = jnp.exp2(dot_nt(nk, nq) * SCALE2) * mask
    return nq, nk, e * (1.0 / jnp.sum(e, axis=0, keepdims=True))


def temporal_value_kernel(gains_ref, mask_ref, got_ref, out_ref):
    gq, gk = gains_ref[2:3, :], gains_ref[3:4, :]
    mask = mask_ref[...]
    for h in range(HEADS):
        at = slice(h * HD, (h + 1) * HD)
        tq, tk, og = [got_ref[:, n, :, at].astype(F32) for n in range(3)]
        parts = []
        for j in range(ROWS // 8):
            qh, _ = unit(cut(tq, j))
            kh, _ = unit(cut(tk, j))
            _, _, w = temporal_weights(qh, kh, gq, gk, mask)
            parts.append(dot_nn(w.astype(BF), cut(og, j).astype(BF)))
        out_ref[:, :, at] = paste(parts)


def temporal_kernel(gains_ref, mask_ref, tq_ref, tk_ref, og_ref, so_ref, out_ref, gg_ref):
    @pl.when(pl.program_id(0) == 0)
    def _():
        gg_ref[...] = jnp.zeros_like(gg_ref)

    gq, gk = gains_ref[2:3, :], gains_ref[3:4, :]
    mask = mask_ref[...]
    tq, tk, og, so = [ref[:, 0].astype(F32) for ref in (tq_ref, tk_ref, og_ref, so_ref)]
    parts = []
    for j in range(ROWS // 8):
        qh, qf = unit(cut(tq, j))
        kh, kf = unit(cut(tk, j))
        g = cut(og, j).astype(BF)
        v = cut(so, j).astype(BF)
        nq, nk, w = temporal_weights(qh, kh, gq, gk, mask)
        o = dot_tn(w.astype(BF), v)
        dw = dot_nt(v, g).astype(BF).astype(F32)
        ds = w * (dw - jnp.sum(dw * w, axis=0, keepdims=True))
        ds = (ds * SCALE).astype(BF)
        dnq = dot_tn(ds, nk).astype(BF).astype(F32)
        dnk = dot_nn(ds, nq).astype(BF).astype(F32)
        dq, sq = unit_back(dnq, qh, qf, gq)
        dk, sk = unit_back(dnk, kh, kf, gk)
        gg_ref[0:1, :] += sq
        gg_ref[1:2, :] += sk
        parts.append([o, dq, dk])
    for n, array in enumerate(zip(*parts)):
        out_ref[:, n] = paste(array)


def finish_kernel(*refs):
    n = len(refs) // 2
    for src, dst in zip(refs[:n], refs[n:]):
        dst[0, 0, LIVE:, :] = jnp.zeros((POS - LIVE, FEAT), BF)
        for x in range(XS):
            part = src[x * ZS : (x + 1) * ZS, 0].astype(F32).reshape(LIVE, COLS)
            dst[0, 0, :LIVE, x * COLS : (x + 1) * COLS] = part.astype(BF)


SMEM = pl.BlockSpec(memory_space=pltpu.SMEM)
PARAMS = pltpu.CompilerParams(vmem_limit_bytes=32 << 20)
WIDE = pltpu.CompilerParams(vmem_limit_bytes=60 << 20)


def cost(flops, arrays):
    return pl.CostEstimate(flops=flops, bytes_accessed=arrays * 2 * LIVE * FEAT, transcendentals=0)


def exchange(values):
    return lax.all_to_all(values, "seq", split_axis=0, concat_axis=0, tiled=True)


def flips(values, axis, masks):
    size = lax.axis_size(axis)
    return [lax.ppermute(values, axis, [(i, i ^ mask) for i in range(size)]) for mask in masks]


def add_flips(values, axis, a, b):
    one, two, both = flips(values, axis, (a, b, a ^ b))
    return (values + one) + (two + both)


def live_block():
    return pl.BlockSpec((1, 1, LIVE, COLS), lambda i: (0, 0, 0, i))


def full_block():
    return pl.BlockSpec((1, 1, POS, COLS), lambda i: (0, 0, 0, i))


def finish(packed, places):
    full = jax.ShapeDtypeStruct((1, 1, POS, FEAT), BF)
    return pl.pallas_call(
        finish_kernel,
        name="finish",
        grid=(1,),
        out_shape=[full] * len(places),
        in_specs=[
            pl.BlockSpec((SEQ, 1, ROWS, COLS), lambda i, n=n: (0, n, 0, 0)) for n in places
        ],
        out_specs=[pl.BlockSpec((1, 1, POS, FEAT), lambda i: (0, 0, 0, 0))] * len(places),
        compiler_params=PARAMS,
        cost_estimate=cost(0, 2 * len(places)),
    )(*[packed] * len(places))


def per_device(sq, sk, sv, tq, tk, og, segment_ids, live_counts, norm_gains):
    me = lax.axis_index("seq").astype(jnp.int32).reshape(1)
    places = (me, segment_ids, live_counts)
    full = jax.ShapeDtypeStruct((1, 1, POS, FEAT), BF)
    packed = jax.ShapeDtypeStruct((SEQ, ROWS, COLS), BF)
    packed3 = jax.ShapeDtypeStruct((SEQ, 3, ROWS, COLS), BF)
    gains_spec = pl.BlockSpec((4, HD), lambda i: (0, 0))
    gg_spec = pl.BlockSpec((2, HD), lambda i: (0, 0))
    gg_shape = jax.ShapeDtypeStruct((2, HD), F32)

    sent = pl.pallas_call(
        pack_kernel,
        name="pack",
        grid=(XS // PACK_XS,),
        out_shape=jax.ShapeDtypeStruct((SEQ, 4, ROWS, COLS), BF),
        in_specs=[SMEM] * 3
        + [gains_spec]
        + [pl.BlockSpec((1, 1, LIVE, PACK_XS * COLS), lambda i: (0, 0, 0, i))] * 6,
        out_specs=pl.BlockSpec((PACK_XS * ZS, 4, ROWS, COLS), lambda i: (i, 0, 0, 0)),
        compiler_params=WIDE,
        cost_estimate=cost(4 * LIVE * LIVE * FEAT, 10),
    )(*places, norm_gains, tq, tk, og, sq, sk, sv)
    got = exchange(sent)

    seg = jnp.repeat(segment_ids[0], 8)
    pos = jnp.arange(SEQ * 8, dtype=jnp.int32) % 8
    mask = (seg[:, None] == seg[None, :]) & (pos[:, None] == pos[None, :])
    got, mask = lax.optimization_barrier((got, mask.astype(F32)))

    def part(n):
        return pl.BlockSpec((SEQ, 1, ROWS, HD), lambda i: (0, n, 0, i))

    temporal_in = [gains_spec, pl.BlockSpec((SEQ * 8, SEQ * 8), lambda i: (0, 0))]
    temporal_in += [part(n) for n in range(4)]
    whole = pl.BlockSpec(memory_space=pltpu.VMEM)
    dso = pl.pallas_call(
        temporal_value_kernel,
        name="temporal_value",
        out_shape=packed,
        in_specs=[whole] * 3,
        out_specs=whole,
        compiler_params=PARAMS,
        cost_estimate=cost(4 * 9 * 256 * 256 * HD, 4),
    )(norm_gains, mask, got)
    got, dso = lax.optimization_barrier((got, dso))
    dso = exchange(dso)

    back, gains_t = pl.pallas_call(
        temporal_kernel,
        name="temporal",
        grid=(HEADS,),
        out_shape=[packed3, gg_shape],
        in_specs=temporal_in,
        out_specs=[pl.BlockSpec((SEQ, 3, ROWS, HD), lambda i: (0, 0, 0, i)), gg_spec],
        compiler_params=PARAMS,
        cost_estimate=cost(12 * 9 * 256 * 256 * HD, 7),
    )(norm_gains, mask, got, got, got, got)
    back, dso = lax.optimization_barrier((back, dso))
    back = exchange(back)

    dsq, dsk, dsv, gains_s = pl.pallas_call(
        spatial_bwd_kernel,
        name="spatial_bwd",
        grid=(XS,),
        out_shape=[full, full, full, gg_shape],
        in_specs=[SMEM] * 3 + [gains_spec] + [live_block()] * 3 + [pl.BlockSpec((ZS, ROWS, COLS), lambda i: (i, 0, 0))],
        out_specs=[full_block()] * 3 + [gg_spec],
        compiler_params=PARAMS,
        cost_estimate=cost(14 * LIVE * LIVE * FEAT, 8),
    )(*places, norm_gains, sq, sk, sv, dso)
    gains = jnp.concatenate([gains_s, gains_t], axis=0)
    gains = gains + flips(gains, "dp", (1,))[0]
    gains = add_flips(gains, "dp", 2, 4)
    gains = add_flips(gains, "seq", 8, 16)
    gains = add_flips(gains, "seq", 1, 4)
    gains, back = lax.optimization_barrier((gains, back))
    gains = gains + flips(gains, "seq", (2,))[0]
    o, dtq, dtk = finish(back, [0, 1, 2])
    return o, dsq, dsk, dsv, dtq, dtk, gains


def solution(mesh):
    big = P("dp", "seq", None, None)
    return jax.shard_map(
        per_device,
        mesh=mesh,
        in_specs=(big,) * 6 + (P("dp", None), P("dp", None), P()),
        out_specs=(big,) * 6 + (P(),),
        check_vma=False,
    )
```

```python
import math

import jax
import jax.numpy as jnp
from jax import lax
from jax.experimental import pallas as pl
from jax.experimental.pallas import tpu as pltpu
from jax.sharding import PartitionSpec as P

HD = 128
POS = 256
LIVE = 192
FEAT = 1536
SEQ = 32
DP = 8
XS = 4
ZS = 8
ROWS = LIVE // ZS
COLS = FEAT // XS
HEADS = COLS // HD
PACK_XS = 2
EPS = 1e-6
SCALE = HD ** -0.5
SCALE2 = SCALE * math.log2(math.e)
BF = jnp.bfloat16
F32 = jnp.float32


def dot_nt(a, b):
    return lax.dot_general(a, b, (((1,), (1,)), ((), ())), preferred_element_type=F32)


def dot_nn(a, b):
    return lax.dot_general(a, b, (((1,), (0,)), ((), ())), preferred_element_type=F32)


def dot_tn(a, b):
    return lax.dot_general(a, b, (((0,), (0,)), ((), ())), preferred_element_type=F32)


def unit(x):
    factor = lax.rsqrt(jnp.mean(x * x, axis=-1, keepdims=True) + EPS)
    return x * factor, factor


def unit_back(grad, hat, factor, gain):
    gd = grad * gain
    dx = factor * (gd - hat * jnp.mean(gd * hat, axis=-1, keepdims=True))
    return dx, jnp.sum(grad * hat, axis=0, keepdims=True)


def count_of(place_ref, seg_ref, counts_ref):
    return counts_ref[0, seg_ref[0, place_ref[0]]]


def spatial_weights(nq, nk, live_keys):
    e = jnp.exp2(dot_nt(nk, nq) * SCALE2)
    e = jnp.where(live_keys, e, 0.0)
    return e * (1.0 / jnp.sum(e, axis=0, keepdims=True))


def pack_kernel(
    me_ref, seg_ref, counts_ref, gains_ref, tq_ref, tk_ref, og_ref, q_ref, k_ref, v_ref, out_ref
):
    count = count_of(me_ref, seg_ref, counts_ref)
    live_rows = lax.broadcasted_iota(jnp.int32, (LIVE, HD), 0) < count
    ones = jnp.where(live_rows, 1.0, 0.0).astype(BF)
    for h in range(HEADS * PACK_XS):
        at = slice(h * HD, (h + 1) * HD)
        x, to = h // HEADS, slice(h % HEADS * HD, (h % HEADS + 1) * HD)

        def put(n, values):
            out_ref[x * ZS : (x + 1) * ZS, n, :, to] = values.reshape(ZS, ROWS, HD).astype(BF)

        put(0, tq_ref[0, 0, :, at].astype(F32))
        put(1, tk_ref[0, 0, :, at].astype(F32))
        put(2, jnp.where(live_rows, og_ref[0, 0, :, at].astype(F32), 0.0))
        qh, _ = unit(q_ref[0, 0, :, at].astype(F32))
        kh, _ = unit(k_ref[0, 0, :, at].astype(F32))
        nq = (qh * gains_ref[0:1, :]).astype(BF)
        nk = (kh * gains_ref[1:2, :]).astype(BF)
        e = jnp.exp2(dot_nt(nq, nk) * SCALE2).astype(BF)
        v = jnp.where(live_rows, v_ref[0, 0, :, at].astype(F32), 0.0).astype(BF)
        both = dot_nn(e, jnp.concatenate([v, ones], axis=1))
        put(3, jnp.where(live_rows, both[:, :HD] * (1.0 / both[:, HD:]), 0.0))


def spatial_bwd_kernel(
    place_ref, seg_ref, counts_ref, gains_ref, q_ref, k_ref, v_ref, g_ref, dq_ref, dk_ref, dv_ref, gg_ref
):
    @pl.when(pl.program_id(0) == 0)
    def _():
        gg_ref[...] = jnp.zeros_like(gg_ref)

    count = count_of(place_ref, seg_ref, counts_ref)
    live_keys = lax.broadcasted_iota(jnp.int32, (LIVE, LIVE), 0) < count
    for ref in (dq_ref, dk_ref, dv_ref):
        ref[0, 0, LIVE:, :] = jnp.zeros((POS - LIVE, COLS), BF)
    for h in range(HEADS):
        at = slice(h * HD, (h + 1) * HD)
        gq, gk = gains_ref[0:1, :], gains_ref[1:2, :]
        qh, qf = unit(q_ref[0, 0, :, at].astype(F32))
        kh, kf = unit(k_ref[0, 0, :, at].astype(F32))
        nq = (qh * gq).astype(BF)
        nk = (kh * gk).astype(BF)
        v = v_ref[0, 0, :, at]
        g = g_ref[:, :, at].astype(F32).reshape(LIVE, HD).astype(BF)
        w = spatial_weights(nq, nk, live_keys)
        dv = dot_nn(w.astype(BF), g)
        dw = dot_nt(v, g).astype(BF).astype(F32)
        ds = w * (dw - jnp.sum(dw * w, axis=0, keepdims=True))
        ds = (ds * SCALE).astype(BF)
        dnq = dot_tn(ds, nk).astype(BF).astype(F32)
        dnk = dot_nn(ds, nq).astype(BF).astype(F32)
        dq, sq = unit_back(dnq, qh, qf, gq)
        dk, sk = unit_back(dnk, kh, kf, gk)
        dq_ref[0, 0, :LIVE, at] = dq.astype(BF)
        dk_ref[0, 0, :LIVE, at] = dk.astype(BF)
        dv_ref[0, 0, :LIVE, at] = dv.astype(BF)
        gg_ref[0:1, :] += sq
        gg_ref[1:2, :] += sk


def cut(a, j):
    return a[:, 8 * j : 8 * j + 8, :].reshape(SEQ * 8, HD)


def paste(parts):
    return jnp.concatenate([a.reshape(SEQ, 8, HD) for a in parts], axis=1).astype(BF)


def temporal_weights(qh, kh, gq, gk, mask):
    nq = (qh * gq).astype(BF)
    nk = (kh * gk).astype(BF)
    e = jnp.exp2(dot_nt(nk, nq) * SCALE2) * mask
    return nq, nk, e * (1.0 / jnp.sum(e, axis=0, keepdims=True))


def temporal_value_kernel(gains_ref, mask_ref, got_ref, out_ref):
    gq, gk = gains_ref[2:3, :], gains_ref[3:4, :]
    mask = mask_ref[...]
    for h in range(HEADS):
        at = slice(h * HD, (h + 1) * HD)
        tq, tk, og = [got_ref[:, n, :, at].astype(F32) for n in range(3)]
        parts = []
        for j in range(ROWS // 8):
            qh, _ = unit(cut(tq, j))
            kh, _ = unit(cut(tk, j))
            _, _, w = temporal_weights(qh, kh, gq, gk, mask)
            parts.append(dot_nn(w.astype(BF), cut(og, j).astype(BF)))
        out_ref[:, :, at] = paste(parts)


def temporal_kernel(gains_ref, mask_ref, tq_ref, tk_ref, og_ref, so_ref, out_ref, gg_ref):
    @pl.when(pl.program_id(0) == 0)
    def _():
        gg_ref[...] = jnp.zeros_like(gg_ref)

    gq, gk = gains_ref[2:3, :], gains_ref[3:4, :]
    mask = mask_ref[...]
    tq, tk, og, so = [ref[:, 0].astype(F32) for ref in (tq_ref, tk_ref, og_ref, so_ref)]
    parts = []
    for j in range(ROWS // 8):
        qh, qf = unit(cut(tq, j))
        kh, kf = unit(cut(tk, j))
        g = cut(og, j).astype(BF)
        v = cut(so, j).astype(BF)
        nq, nk, w = temporal_weights(qh, kh, gq, gk, mask)
        o = dot_tn(w.astype(BF), v)
        dw = dot_nt(v, g).astype(BF).astype(F32)
        ds = w * (dw - jnp.sum(dw * w, axis=0, keepdims=True))
        ds = (ds * SCALE).astype(BF)
        dnq = dot_tn(ds, nk).astype(BF).astype(F32)
        dnk = dot_nn(ds, nq).astype(BF).astype(F32)
        dq, sq = unit_back(dnq, qh, qf, gq)
        dk, sk = unit_back(dnk, kh, kf, gk)
        gg_ref[0:1, :] += sq
        gg_ref[1:2, :] += sk
        parts.append([o, dq, dk])
    for n, array in enumerate(zip(*parts)):
        out_ref[:, n] = paste(array)


def finish_kernel(*refs):
    n = len(refs) // 2
    for src, dst in zip(refs[:n], refs[n:]):
        dst[0, 0, LIVE:, :] = jnp.zeros((POS - LIVE, FEAT), BF)
        for x in range(XS):
            part = src[x * ZS : (x + 1) * ZS, 0].astype(F32).reshape(LIVE, COLS)
            dst[0, 0, :LIVE, x * COLS : (x + 1) * COLS] = part.astype(BF)


SMEM = pl.BlockSpec(memory_space=pltpu.SMEM)
PARAMS = pltpu.CompilerParams(vmem_limit_bytes=32 << 20)
WIDE = pltpu.CompilerParams(vmem_limit_bytes=60 << 20)


def cost(flops, arrays):
    return pl.CostEstimate(flops=flops, bytes_accessed=arrays * 2 * LIVE * FEAT, transcendentals=0)


def exchange(values):
    return lax.all_to_all(values, "seq", split_axis=0, concat_axis=0, tiled=True)


def flips(values, axis, masks):
    size = lax.axis_size(axis)
    return [lax.ppermute(values, axis, [(i, i ^ mask) for i in range(size)]) for mask in masks]


def add_flips(values, axis, a, b):
    one, two, both = flips(values, axis, (a, b, a ^ b))
    return (values + one) + (two + both)


def live_block():
    return pl.BlockSpec((1, 1, LIVE, COLS), lambda i: (0, 0, 0, i))


def full_block():
    return pl.BlockSpec((1, 1, POS, COLS), lambda i: (0, 0, 0, i))


def finish(packed, places):
    full = jax.ShapeDtypeStruct((1, 1, POS, FEAT), BF)
    return pl.pallas_call(
        finish_kernel,
        name="finish",
        grid=(1,),
        out_shape=[full] * len(places),
        in_specs=[
            pl.BlockSpec((SEQ, 1, ROWS, COLS), lambda i, n=n: (0, n, 0, 0)) for n in places
        ],
        out_specs=[pl.BlockSpec((1, 1, POS, FEAT), lambda i: (0, 0, 0, 0))] * len(places),
        compiler_params=PARAMS,
        cost_estimate=cost(0, 2 * len(places)),
    )(*[packed] * len(places))


def per_device(sq, sk, sv, tq, tk, og, segment_ids, live_counts, norm_gains):
    me = lax.axis_index("seq").astype(jnp.int32).reshape(1)
    places = (me, segment_ids, live_counts)
    full = jax.ShapeDtypeStruct((1, 1, POS, FEAT), BF)
    packed = jax.ShapeDtypeStruct((SEQ, ROWS, COLS), BF)
    packed3 = jax.ShapeDtypeStruct((SEQ, 3, ROWS, COLS), BF)
    gains_spec = pl.BlockSpec((4, HD), lambda i: (0, 0))
    gg_spec = pl.BlockSpec((2, HD), lambda i: (0, 0))
    gg_shape = jax.ShapeDtypeStruct((2, HD), F32)

    sent = pl.pallas_call(
        pack_kernel,
        name="pack",
        grid=(XS // PACK_XS,),
        out_shape=jax.ShapeDtypeStruct((SEQ, 4, ROWS, COLS), BF),
        in_specs=[SMEM] * 3
        + [gains_spec]
        + [pl.BlockSpec((1, 1, LIVE, PACK_XS * COLS), lambda i: (0, 0, 0, i))] * 6,
        out_specs=pl.BlockSpec((PACK_XS * ZS, 4, ROWS, COLS), lambda i: (i, 0, 0, 0)),
        compiler_params=WIDE,
        cost_estimate=cost(4 * LIVE * LIVE * FEAT, 10),
    )(*places, norm_gains, tq, tk, og, sq, sk, sv)
    got = exchange(sent)

    seg = jnp.repeat(segment_ids[0], 8)
    pos = jnp.arange(SEQ * 8, dtype=jnp.int32) % 8
    mask = (seg[:, None] == seg[None, :]) & (pos[:, None] == pos[None, :])
    got, mask = lax.optimization_barrier((got, mask.astype(F32)))

    def part(n):
        return pl.BlockSpec((SEQ, 1, ROWS, HD), lambda i: (0, n, 0, i))

    temporal_in = [gains_spec, pl.BlockSpec((SEQ * 8, SEQ * 8), lambda i: (0, 0))]
    temporal_in += [part(n) for n in range(4)]
    whole = pl.BlockSpec(memory_space=pltpu.VMEM)
    dso = pl.pallas_call(
        temporal_value_kernel,
        name="temporal_value",
        out_shape=packed,
        in_specs=[whole] * 3,
        out_specs=whole,
        compiler_params=PARAMS,
        cost_estimate=cost(4 * 9 * 256 * 256 * HD, 4),
    )(norm_gains, mask, got)
    got, dso = lax.optimization_barrier((got, dso))
    dso = exchange(dso)

    back, gains_t = pl.pallas_call(
        temporal_kernel,
        name="temporal",
        grid=(HEADS,),
        out_shape=[packed3, gg_shape],
        in_specs=temporal_in,
        out_specs=[pl.BlockSpec((SEQ, 3, ROWS, HD), lambda i: (0, 0, 0, i)), gg_spec],
        compiler_params=PARAMS,
        cost_estimate=cost(12 * 9 * 256 * 256 * HD, 7),
    )(norm_gains, mask, got, got, got, got)
    back, dso = lax.optimization_barrier((back, dso))
    back = exchange(back)

    dsq, dsk, dsv, gains_s = pl.pallas_call(
        spatial_bwd_kernel,
        name="spatial_bwd",
        grid=(XS,),
        out_shape=[full, full, full, gg_shape],
        in_specs=[SMEM] * 3 + [gains_spec] + [live_block()] * 3 + [pl.BlockSpec((ZS, ROWS, COLS), lambda i: (i, 0, 0))],
        out_specs=[full_block()] * 3 + [gg_spec],
        compiler_params=PARAMS,
        cost_estimate=cost(14 * LIVE * LIVE * FEAT, 8),
    )(*places, norm_gains, sq, sk, sv, dso)
    gains = jnp.concatenate([gains_s, gains_t], axis=0)
    gains = gains + flips(gains, "dp", (1,))[0]
    gains = add_flips(gains, "dp", 2, 4)
    gains = add_flips(gains, "seq", 8, 16)
    gains = add_flips(gains, "seq", 2, 4)
    gains, back = lax.optimization_barrier((gains, back))
    gains = gains + flips(gains, "seq", (1,))[0]
    o, dtq, dtk = finish(back, [0, 1, 2])
    return o, dsq, dsk, dsv, dtq, dtk, gains


def solution(mesh):
    big = P("dp", "seq", None, None)
    return jax.shard_map(
        per_device,
        mesh=mesh,
        in_specs=(big,) * 6 + (P("dp", None), P("dp", None), P()),
        out_specs=(big,) * 6 + (P(),),
        check_vma=False,
    )
```

```python
import math

import jax
import jax.numpy as jnp
from jax import lax
from jax.experimental import pallas as pl
from jax.experimental.pallas import tpu as pltpu
from jax.sharding import PartitionSpec as P

HD = 128
POS = 256
LIVE = 192
FEAT = 1536
SEQ = 32
DP = 8
XS = 4
ZS = 8
ROWS = LIVE // ZS
COLS = FEAT // XS
HEADS = COLS // HD
PACK_XS = 2
EPS = 1e-6
SCALE = HD ** -0.5
SCALE2 = SCALE * math.log2(math.e)
BF = jnp.bfloat16
F32 = jnp.float32


def dot_nt(a, b):
    return lax.dot_general(a, b, (((1,), (1,)), ((), ())), preferred_element_type=F32)


def dot_nn(a, b):
    return lax.dot_general(a, b, (((1,), (0,)), ((), ())), preferred_element_type=F32)


def dot_tn(a, b):
    return lax.dot_general(a, b, (((0,), (0,)), ((), ())), preferred_element_type=F32)


def unit(x):
    factor = lax.rsqrt(jnp.mean(x * x, axis=-1, keepdims=True) + EPS)
    return x * factor, factor


def unit_back(grad, hat, factor, gain):
    gd = grad * gain
    dx = factor * (gd - hat * jnp.mean(gd * hat, axis=-1, keepdims=True))
    return dx, jnp.sum(grad * hat, axis=0, keepdims=True)


def count_of(place_ref, seg_ref, counts_ref):
    return counts_ref[0, seg_ref[0, place_ref[0]]]


def spatial_weights(nq, nk, live_keys):
    e = jnp.exp2(dot_nt(nk, nq) * SCALE2)
    e = jnp.where(live_keys, e, 0.0)
    return e * (1.0 / jnp.sum(e, axis=0, keepdims=True))


def pack_kernel(
    me_ref, seg_ref, counts_ref, gains_ref, tq_ref, tk_ref, og_ref, q_ref, k_ref, v_ref, out_ref
):
    count = count_of(me_ref, seg_ref, counts_ref)
    live_rows = lax.broadcasted_iota(jnp.int32, (LIVE, HD), 0) < count
    ones = jnp.where(live_rows, 1.0, 0.0).astype(BF)
    for h in range(HEADS * PACK_XS):
        at = slice(h * HD, (h + 1) * HD)
        x, to = h // HEADS, slice(h % HEADS * HD, (h % HEADS + 1) * HD)

        def put(n, values):
            out_ref[x * ZS : (x + 1) * ZS, n, :, to] = values.reshape(ZS, ROWS, HD).astype(BF)

        put(0, tq_ref[0, 0, :, at].astype(F32))
        put(1, tk_ref[0, 0, :, at].astype(F32))
        put(2, jnp.where(live_rows, og_ref[0, 0, :, at].astype(F32), 0.0))
        qh, _ = unit(q_ref[0, 0, :, at].astype(F32))
        kh, _ = unit(k_ref[0, 0, :, at].astype(F32))
        nq = (qh * gains_ref[0:1, :]).astype(BF)
        nk = (kh * gains_ref[1:2, :]).astype(BF)
        e = jnp.exp2(dot_nt(nq, nk) * SCALE2).astype(BF)
        v = jnp.where(live_rows, v_ref[0, 0, :, at].astype(F32), 0.0).astype(BF)
        both = dot_nn(e, jnp.concatenate([v, ones], axis=1))
        put(3, jnp.where(live_rows, both[:, :HD] * (1.0 / both[:, HD:]), 0.0))


def spatial_bwd_kernel(
    place_ref, seg_ref, counts_ref, gains_ref, q_ref, k_ref, v_ref, g_ref, dq_ref, dk_ref, dv_ref, gg_ref
):
    @pl.when(pl.program_id(0) == 0)
    def _():
        gg_ref[...] = jnp.zeros_like(gg_ref)

    count = count_of(place_ref, seg_ref, counts_ref)
    live_keys = lax.broadcasted_iota(jnp.int32, (LIVE, LIVE), 0) < count
    for ref in (dq_ref, dk_ref, dv_ref):
        ref[0, 0, LIVE:, :] = jnp.zeros((POS - LIVE, PACK_XS * COLS), BF)
    for h in range(HEADS * PACK_XS):
        at = slice(h * HD, (h + 1) * HD)
        x, to = h // HEADS, slice(h % HEADS * HD, (h % HEADS + 1) * HD)
        gq, gk = gains_ref[0:1, :], gains_ref[1:2, :]
        qh, qf = unit(q_ref[0, 0, :, at].astype(F32))
        kh, kf = unit(k_ref[0, 0, :, at].astype(F32))
        nq = (qh * gq).astype(BF)
        nk = (kh * gk).astype(BF)
        v = v_ref[0, 0, :, at]
        g = g_ref[x * ZS : (x + 1) * ZS, :, to].astype(F32).reshape(LIVE, HD).astype(BF)
        w = spatial_weights(nq, nk, live_keys)
        dv = dot_nn(w.astype(BF), g)
        dw = dot_nt(v, g).astype(BF).astype(F32)
        ds = w * (dw - jnp.sum(dw * w, axis=0, keepdims=True))
        ds = (ds * SCALE).astype(BF)
        dnq = dot_tn(ds, nk).astype(BF).astype(F32)
        dnk = dot_nn(ds, nq).astype(BF).astype(F32)
        dq, sq = unit_back(dnq, qh, qf, gq)
        dk, sk = unit_back(dnk, kh, kf, gk)
        dq_ref[0, 0, :LIVE, at] = dq.astype(BF)
        dk_ref[0, 0, :LIVE, at] = dk.astype(BF)
        dv_ref[0, 0, :LIVE, at] = dv.astype(BF)
        gg_ref[0:1, :] += sq
        gg_ref[1:2, :] += sk


def cut(a, j):
    return a[:, 8 * j : 8 * j + 8, :].reshape(SEQ * 8, HD)


def paste(parts):
    return jnp.concatenate([a.reshape(SEQ, 8, HD) for a in parts], axis=1).astype(BF)


def temporal_weights(qh, kh, gq, gk, mask):
    nq = (qh * gq).astype(BF)
    nk = (kh * gk).astype(BF)
    e = jnp.exp2(dot_nt(nk, nq) * SCALE2) * mask
    return nq, nk, e * (1.0 / jnp.sum(e, axis=0, keepdims=True))


def temporal_value_kernel(gains_ref, mask_ref, got_ref, out_ref):
    gq, gk = gains_ref[2:3, :], gains_ref[3:4, :]
    mask = mask_ref[...]
    for h in range(HEADS):
        at = slice(h * HD, (h + 1) * HD)
        tq, tk, og = [got_ref[:, n, :, at].astype(F32) for n in range(3)]
        parts = []
        for j in range(ROWS // 8):
            qh, _ = unit(cut(tq, j))
            kh, _ = unit(cut(tk, j))
            _, _, w = temporal_weights(qh, kh, gq, gk, mask)
            parts.append(dot_nn(w.astype(BF), cut(og, j).astype(BF)))
        out_ref[:, :, at] = paste(parts)


def temporal_kernel(gains_ref, mask_ref, tq_ref, tk_ref, og_ref, so_ref, out_ref, gg_ref):
    @pl.when(pl.program_id(0) == 0)
    def _():
        gg_ref[...] = jnp.zeros_like(gg_ref)

    gq, gk = gains_ref[2:3, :], gains_ref[3:4, :]
    mask = mask_ref[...]
    tq, tk, og, so = [ref[:, 0].astype(F32) for ref in (tq_ref, tk_ref, og_ref, so_ref)]
    parts = []
    for j in range(ROWS // 8):
        qh, qf = unit(cut(tq, j))
        kh, kf = unit(cut(tk, j))
        g = cut(og, j).astype(BF)
        v = cut(so, j).astype(BF)
        nq, nk, w = temporal_weights(qh, kh, gq, gk, mask)
        o = dot_tn(w.astype(BF), v)
        dw = dot_nt(v, g).astype(BF).astype(F32)
        ds = w * (dw - jnp.sum(dw * w, axis=0, keepdims=True))
        ds = (ds * SCALE).astype(BF)
        dnq = dot_tn(ds, nk).astype(BF).astype(F32)
        dnk = dot_nn(ds, nq).astype(BF).astype(F32)
        dq, sq = unit_back(dnq, qh, qf, gq)
        dk, sk = unit_back(dnk, kh, kf, gk)
        gg_ref[0:1, :] += sq
        gg_ref[1:2, :] += sk
        parts.append([o, dq, dk])
    for n, array in enumerate(zip(*parts)):
        out_ref[:, n] = paste(array)


def finish_kernel(*refs):
    n = len(refs) // 2
    for src, dst in zip(refs[:n], refs[n:]):
        dst[0, 0, LIVE:, :] = jnp.zeros((POS - LIVE, FEAT), BF)
        for x in range(XS):
            part = src[x * ZS : (x + 1) * ZS, 0].astype(F32).reshape(LIVE, COLS)
            dst[0, 0, :LIVE, x * COLS : (x + 1) * COLS] = part.astype(BF)


SMEM = pl.BlockSpec(memory_space=pltpu.SMEM)
PARAMS = pltpu.CompilerParams(vmem_limit_bytes=32 << 20)
WIDE = pltpu.CompilerParams(vmem_limit_bytes=60 << 20)


def cost(flops, arrays):
    return pl.CostEstimate(flops=flops, bytes_accessed=arrays * 2 * LIVE * FEAT, transcendentals=0)


def exchange(values):
    return lax.all_to_all(values, "seq", split_axis=0, concat_axis=0, tiled=True)


def flips(values, axis, masks):
    size = lax.axis_size(axis)
    return [lax.ppermute(values, axis, [(i, i ^ mask) for i in range(size)]) for mask in masks]


def add_flips(values, axis, a, b):
    one, two, both = flips(values, axis, (a, b, a ^ b))
    return (values + one) + (two + both)


def wide_block(rows):
    return pl.BlockSpec((1, 1, rows, PACK_XS * COLS), lambda i: (0, 0, 0, i))


def finish(packed, places):
    full = jax.ShapeDtypeStruct((1, 1, POS, FEAT), BF)
    return pl.pallas_call(
        finish_kernel,
        name="finish",
        grid=(1,),
        out_shape=[full] * len(places),
        in_specs=[
            pl.BlockSpec((SEQ, 1, ROWS, COLS), lambda i, n=n: (0, n, 0, 0)) for n in places
        ],
        out_specs=[pl.BlockSpec((1, 1, POS, FEAT), lambda i: (0, 0, 0, 0))] * len(places),
        compiler_params=PARAMS,
        cost_estimate=cost(0, 2 * len(places)),
    )(*[packed] * len(places))


def per_device(sq, sk, sv, tq, tk, og, segment_ids, live_counts, norm_gains):
    me = lax.axis_index("seq").astype(jnp.int32).reshape(1)
    places = (me, segment_ids, live_counts)
    full = jax.ShapeDtypeStruct((1, 1, POS, FEAT), BF)
    packed = jax.ShapeDtypeStruct((SEQ, ROWS, COLS), BF)
    packed3 = jax.ShapeDtypeStruct((SEQ, 3, ROWS, COLS), BF)
    gains_spec = pl.BlockSpec((4, HD), lambda i: (0, 0))
    gg_spec = pl.BlockSpec((2, HD), lambda i: (0, 0))
    gg_shape = jax.ShapeDtypeStruct((2, HD), F32)

    sent = pl.pallas_call(
        pack_kernel,
        name="pack",
        grid=(XS // PACK_XS,),
        out_shape=jax.ShapeDtypeStruct((SEQ, 4, ROWS, COLS), BF),
        in_specs=[SMEM] * 3
        + [gains_spec]
        + [wide_block(LIVE)] * 6,
        out_specs=pl.BlockSpec((PACK_XS * ZS, 4, ROWS, COLS), lambda i: (i, 0, 0, 0)),
        compiler_params=WIDE,
        cost_estimate=cost(4 * LIVE * LIVE * FEAT, 10),
    )(*places, norm_gains, tq, tk, og, sq, sk, sv)
    got = exchange(sent)

    seg = jnp.repeat(segment_ids[0], 8)
    pos = jnp.arange(SEQ * 8, dtype=jnp.int32) % 8
    mask = (seg[:, None] == seg[None, :]) & (pos[:, None] == pos[None, :])
    got, mask = lax.optimization_barrier((got, mask.astype(F32)))

    def part(n):
        return pl.BlockSpec((SEQ, 1, ROWS, HD), lambda i: (0, n, 0, i))

    temporal_in = [gains_spec, pl.BlockSpec((SEQ * 8, SEQ * 8), lambda i: (0, 0))]
    temporal_in += [part(n) for n in range(4)]
    whole = pl.BlockSpec(memory_space=pltpu.VMEM)
    dso = pl.pallas_call(
        temporal_value_kernel,
        name="temporal_value",
        out_shape=packed,
        in_specs=[whole] * 3,
        out_specs=whole,
        compiler_params=PARAMS,
        cost_estimate=cost(4 * 9 * 256 * 256 * HD, 4),
    )(norm_gains, mask, got)
    got, dso = lax.optimization_barrier((got, dso))
    dso = exchange(dso)

    back, gains_t = pl.pallas_call(
        temporal_kernel,
        name="temporal",
        grid=(HEADS,),
        out_shape=[packed3, gg_shape],
        in_specs=temporal_in,
        out_specs=[pl.BlockSpec((SEQ, 3, ROWS, HD), lambda i: (0, 0, 0, i)), gg_spec],
        compiler_params=PARAMS,
        cost_estimate=cost(12 * 9 * 256 * 256 * HD, 7),
    )(norm_gains, mask, got, got, got, got)
    back, dso = lax.optimization_barrier((back, dso))
    back = exchange(back)

    dsq, dsk, dsv, gains_s = pl.pallas_call(
        spatial_bwd_kernel,
        name="spatial_bwd",
        grid=(XS // PACK_XS,),
        out_shape=[full, full, full, gg_shape],
        in_specs=[SMEM] * 3
        + [gains_spec]
        + [wide_block(LIVE)] * 3
        + [pl.BlockSpec((PACK_XS * ZS, ROWS, COLS), lambda i: (i, 0, 0))],
        out_specs=[wide_block(POS)] * 3 + [gg_spec],
        compiler_params=PARAMS,
        cost_estimate=cost(14 * LIVE * LIVE * FEAT, 8),
    )(*places, norm_gains, sq, sk, sv, dso)
    gains = jnp.concatenate([gains_s, gains_t], axis=0)
    gains = gains + flips(gains, "dp", (1,))[0]
    gains = add_flips(gains, "dp", 2, 4)
    gains = add_flips(gains, "seq", 8, 16)
    gains = add_flips(gains, "seq", 2, 4)
    gains, back = lax.optimization_barrier((gains, back))
    gains = gains + flips(gains, "seq", (1,))[0]
    o, dtq, dtk = finish(back, [0, 1, 2])
    return o, dsq, dsk, dsv, dtq, dtk, gains


def solution(mesh):
    big = P("dp", "seq", None, None)
    return jax.shard_map(
        per_device,
        mesh=mesh,
        in_specs=(big,) * 6 + (P("dp", None), P("dp", None), P()),
        out_specs=(big,) * 6 + (P(),),
        check_vma=False,
    )
```

```python
import math

import jax
import jax.numpy as jnp
from jax import lax
from jax.experimental import pallas as pl
from jax.experimental.pallas import tpu as pltpu
from jax.sharding import PartitionSpec as P

HD = 128
POS = 256
LIVE = 192
FEAT = 1536
SEQ = 32
DP = 8
XS = 4
ZS = 8
ROWS = LIVE // ZS
COLS = FEAT // XS
HEADS = COLS // HD
PACK_XS = 2
EPS = 1e-6
SCALE = HD ** -0.5
SCALE2 = SCALE * math.log2(math.e)
BF = jnp.bfloat16
F32 = jnp.float32


def dot_nt(a, b):
    return lax.dot_general(a, b, (((1,), (1,)), ((), ())), preferred_element_type=F32)


def dot_nn(a, b):
    return lax.dot_general(a, b, (((1,), (0,)), ((), ())), preferred_element_type=F32)


def dot_tn(a, b):
    return lax.dot_general(a, b, (((0,), (0,)), ((), ())), preferred_element_type=F32)


def unit(x):
    factor = lax.rsqrt(jnp.mean(x * x, axis=-1, keepdims=True) + EPS)
    return x * factor, factor


def unit_back(grad, hat, factor, gain):
    gd = grad * gain
    dx = factor * (gd - hat * jnp.mean(gd * hat, axis=-1, keepdims=True))
    return dx, jnp.sum(grad * hat, axis=0, keepdims=True)


def count_of(place_ref, seg_ref, counts_ref):
    return counts_ref[0, seg_ref[0, place_ref[0]]]


def spatial_weights(nq, nk, live_keys):
    e = jnp.exp2(dot_nt(nk, nq) * SCALE2)
    e = jnp.where(live_keys, e, 0.0)
    return e * (1.0 / jnp.sum(e, axis=0, keepdims=True))


def pack_kernel(
    me_ref, seg_ref, counts_ref, gains_ref, tq_ref, tk_ref, og_ref, q_ref, k_ref, v_ref, out_ref
):
    count = count_of(me_ref, seg_ref, counts_ref)
    live_rows = lax.broadcasted_iota(jnp.int32, (LIVE, HD), 0) < count
    ones = jnp.where(live_rows, 1.0, 0.0).astype(BF)
    for h in range(HEADS * PACK_XS):
        at = slice(h * HD, (h + 1) * HD)
        x, to = h // HEADS, slice(h % HEADS * HD, (h % HEADS + 1) * HD)

        def put(n, values):
            out_ref[x * ZS : (x + 1) * ZS, n, :, to] = values.reshape(ZS, ROWS, HD).astype(BF)

        put(0, tq_ref[0, 0, :, at].astype(F32))
        put(1, tk_ref[0, 0, :, at].astype(F32))
        put(2, jnp.where(live_rows, og_ref[0, 0, :, at].astype(F32), 0.0))
        qh, _ = unit(q_ref[0, 0, :, at].astype(F32))
        kh, _ = unit(k_ref[0, 0, :, at].astype(F32))
        nq = (qh * gains_ref[0:1, :]).astype(BF)
        nk = (kh * gains_ref[1:2, :]).astype(BF)
        e = jnp.exp2(dot_nt(nq, nk) * SCALE2).astype(BF)
        v = jnp.where(live_rows, v_ref[0, 0, :, at].astype(F32), 0.0).astype(BF)
        both = dot_nn(e, jnp.concatenate([v, ones], axis=1))
        put(3, jnp.where(live_rows, both[:, :HD] * (1.0 / both[:, HD:]), 0.0))


def spatial_bwd_kernel(
    place_ref, seg_ref, counts_ref, gains_ref, q_ref, k_ref, v_ref, g_ref, dq_ref, dk_ref, dv_ref, gg_ref
):
    @pl.when(pl.program_id(0) == 0)
    def _():
        gg_ref[...] = jnp.zeros_like(gg_ref)

    count = count_of(place_ref, seg_ref, counts_ref)
    live_keys = lax.broadcasted_iota(jnp.int32, (LIVE, LIVE), 0) < count
    for ref in (dq_ref, dk_ref, dv_ref):
        ref[0, 0, LIVE:, :] = jnp.zeros((POS - LIVE, PACK_XS * COLS), BF)
    for h in range(HEADS * PACK_XS):
        at = slice(h * HD, (h + 1) * HD)
        x, to = h // HEADS, slice(h % HEADS * HD, (h % HEADS + 1) * HD)
        gq, gk = gains_ref[0:1, :], gains_ref[1:2, :]
        qh, qf = unit(q_ref[0, 0, :, at].astype(F32))
        kh, kf = unit(k_ref[0, 0, :, at].astype(F32))
        nq = (qh * gq).astype(BF)
        nk = (kh * gk).astype(BF)
        v = v_ref[0, 0, :, at]
        g = g_ref[x * ZS : (x + 1) * ZS, :, to].astype(F32).reshape(LIVE, HD).astype(BF)
        w = spatial_weights(nq, nk, live_keys)
        dv = dot_nn(w.astype(BF), g)
        dw = dot_nt(v, g).astype(BF).astype(F32)
        ds = w * (dw - jnp.sum(dw * w, axis=0, keepdims=True))
        ds = (ds * SCALE).astype(BF)
        dnq = dot_tn(ds, nk).astype(BF).astype(F32)
        dnk = dot_nn(ds, nq).astype(BF).astype(F32)
        dq, sq = unit_back(dnq, qh, qf, gq)
        dk, sk = unit_back(dnk, kh, kf, gk)
        dq_ref[0, 0, :LIVE, at] = dq.astype(BF)
        dk_ref[0, 0, :LIVE, at] = dk.astype(BF)
        dv_ref[0, 0, :LIVE, at] = dv.astype(BF)
        gg_ref[0:1, :] += sq
        gg_ref[1:2, :] += sk


def cut(a, j):
    return a[:, 8 * j : 8 * j + 8, :].reshape(SEQ * 8, HD)


def paste(parts):
    return jnp.concatenate([a.reshape(SEQ, 8, HD) for a in parts], axis=1).astype(BF)


def temporal_weights(qh, kh, gq, gk, mask):
    nq = (qh * gq).astype(BF)
    nk = (kh * gk).astype(BF)
    e = jnp.exp2(dot_nt(nk, nq) * SCALE2) * mask
    return nq, nk, e * (1.0 / jnp.sum(e, axis=0, keepdims=True))


def temporal_value_kernel(gains_ref, mask_ref, got_ref, out_ref):
    gq, gk = gains_ref[2:3, :], gains_ref[3:4, :]
    mask = mask_ref[...]
    for h in range(HEADS):
        at = slice(h * HD, (h + 1) * HD)
        tq, tk, og = [got_ref[:, n, :, at].astype(F32) for n in range(3)]
        parts = []
        for j in range(ROWS // 8):
            qh, _ = unit(cut(tq, j))
            kh, _ = unit(cut(tk, j))
            _, _, w = temporal_weights(qh, kh, gq, gk, mask)
            parts.append(dot_nn(w.astype(BF), cut(og, j).astype(BF)))
        out_ref[:, :, at] = paste(parts)


def temporal_kernel(gains_ref, mask_ref, tq_ref, tk_ref, og_ref, so_ref, out_ref, gg_ref):
    @pl.when(pl.program_id(0) == 0)
    def _():
        gg_ref[...] = jnp.zeros_like(gg_ref)

    gq, gk = gains_ref[2:3, :], gains_ref[3:4, :]
    mask = mask_ref[...]
    tq, tk, og, so = [ref[:, 0].astype(F32) for ref in (tq_ref, tk_ref, og_ref, so_ref)]
    parts = []
    for j in range(ROWS // 8):
        qh, qf = unit(cut(tq, j))
        kh, kf = unit(cut(tk, j))
        g = cut(og, j).astype(BF)
        v = cut(so, j).astype(BF)
        nq, nk, w = temporal_weights(qh, kh, gq, gk, mask)
        o = dot_tn(w.astype(BF), v)
        dw = dot_nt(v, g).astype(BF).astype(F32)
        ds = w * (dw - jnp.sum(dw * w, axis=0, keepdims=True))
        ds = (ds * SCALE).astype(BF)
        dnq = dot_tn(ds, nk).astype(BF).astype(F32)
        dnk = dot_nn(ds, nq).astype(BF).astype(F32)
        dq, sq = unit_back(dnq, qh, qf, gq)
        dk, sk = unit_back(dnk, kh, kf, gk)
        gg_ref[0:1, :] += sq
        gg_ref[1:2, :] += sk
        parts.append([o, dq, dk])
    for n, array in enumerate(zip(*parts)):
        out_ref[:, n] = paste(array)


def finish_kernel(*refs):
    n = len(refs) // 2
    for src, dst in zip(refs[:n], refs[n:]):
        dst[0, 0, LIVE:, :] = jnp.zeros((POS - LIVE, FEAT), BF)
        for x in range(XS):
            part = src[x * ZS : (x + 1) * ZS, 0].astype(F32).reshape(LIVE, COLS)
            dst[0, 0, :LIVE, x * COLS : (x + 1) * COLS] = part.astype(BF)


SMEM = pl.BlockSpec(memory_space=pltpu.SMEM)
PARAMS = pltpu.CompilerParams(vmem_limit_bytes=32 << 20)
WIDE = pltpu.CompilerParams(vmem_limit_bytes=60 << 20)


def cost(flops, arrays):
    return pl.CostEstimate(flops=flops, bytes_accessed=arrays * 2 * LIVE * FEAT, transcendentals=0)


def exchange(values):
    return lax.all_to_all(values, "seq", split_axis=0, concat_axis=0, tiled=True)


def flips(values, axis, masks):
    size = lax.axis_size(axis)
    return [lax.ppermute(values, axis, [(i, i ^ mask) for i in range(size)]) for mask in masks]


def add_flips(values, axis, a, b):
    one, two, both = flips(values, axis, (a, b, a ^ b))
    return (values + one) + (two + both)


def wide_block(rows):
    return pl.BlockSpec((1, 1, rows, PACK_XS * COLS), lambda i: (0, 0, 0, i))


def finish(packed, places):
    full = jax.ShapeDtypeStruct((1, 1, POS, FEAT), BF)
    return pl.pallas_call(
        finish_kernel,
        name="finish",
        grid=(1,),
        out_shape=[full] * len(places),
        in_specs=[
            pl.BlockSpec((SEQ, 1, ROWS, COLS), lambda i, n=n: (0, n, 0, 0)) for n in places
        ],
        out_specs=[pl.BlockSpec((1, 1, POS, FEAT), lambda i: (0, 0, 0, 0))] * len(places),
        compiler_params=PARAMS,
        cost_estimate=cost(0, 2 * len(places)),
    )(*[packed] * len(places))


def per_device(sq, sk, sv, tq, tk, og, segment_ids, live_counts, norm_gains):
    me = lax.axis_index("seq").astype(jnp.int32).reshape(1)
    places = (me, segment_ids, live_counts)
    full = jax.ShapeDtypeStruct((1, 1, POS, FEAT), BF)
    packed = jax.ShapeDtypeStruct((SEQ, ROWS, COLS), BF)
    packed3 = jax.ShapeDtypeStruct((SEQ, 3, ROWS, COLS), BF)
    gains_spec = pl.BlockSpec((4, HD), lambda i: (0, 0))
    gg_spec = pl.BlockSpec((2, HD), lambda i: (0, 0))
    gg_shape = jax.ShapeDtypeStruct((2, HD), F32)

    sent = pl.pallas_call(
        pack_kernel,
        name="pack",
        grid=(XS // PACK_XS,),
        out_shape=jax.ShapeDtypeStruct((SEQ, 4, ROWS, COLS), BF),
        in_specs=[SMEM] * 3
        + [gains_spec]
        + [wide_block(LIVE)] * 6,
        out_specs=pl.BlockSpec((PACK_XS * ZS, 4, ROWS, COLS), lambda i: (i, 0, 0, 0)),
        compiler_params=WIDE,
        cost_estimate=cost(4 * LIVE * LIVE * FEAT, 10),
    )(*places, norm_gains, tq, tk, og, sq, sk, sv)
    got = exchange(sent)

    seg = jnp.repeat(segment_ids[0], 8)
    pos = jnp.arange(SEQ * 8, dtype=jnp.int32) % 8
    mask = (seg[:, None] == seg[None, :]) & (pos[:, None] == pos[None, :])
    got, mask = lax.optimization_barrier((got, mask.astype(F32)))

    def part(n):
        return pl.BlockSpec((SEQ, 1, ROWS, HD), lambda i: (0, n, 0, i))

    temporal_in = [gains_spec, pl.BlockSpec((SEQ * 8, SEQ * 8), lambda i: (0, 0))]
    temporal_in += [part(n) for n in range(4)]
    whole = pl.BlockSpec(memory_space=pltpu.VMEM)
    dso = pl.pallas_call(
        temporal_value_kernel,
        name="temporal_value",
        out_shape=packed,
        in_specs=[whole] * 3,
        out_specs=whole,
        compiler_params=PARAMS,
        cost_estimate=cost(4 * 9 * 256 * 256 * HD, 4),
    )(norm_gains, mask, got)
    got, dso = lax.optimization_barrier((got, dso))
    dso = exchange(dso)

    back, gains_t = pl.pallas_call(
        temporal_kernel,
        name="temporal",
        grid=(HEADS,),
        out_shape=[packed3, gg_shape],
        in_specs=temporal_in,
        out_specs=[pl.BlockSpec((SEQ, 3, ROWS, HD), lambda i: (0, 0, 0, i)), gg_spec],
        compiler_params=PARAMS,
        cost_estimate=cost(12 * 9 * 256 * 256 * HD, 7),
    )(norm_gains, mask, got, got, got, got)
    back, dso = lax.optimization_barrier((back, dso))
    back = exchange(back)

    dsq, dsk, dsv, gains_s = pl.pallas_call(
        spatial_bwd_kernel,
        name="spatial_bwd",
        grid=(XS // PACK_XS,),
        out_shape=[full, full, full, gg_shape],
        in_specs=[SMEM] * 3
        + [gains_spec]
        + [wide_block(LIVE)] * 3
        + [pl.BlockSpec((PACK_XS * ZS, ROWS, COLS), lambda i: (i, 0, 0))],
        out_specs=[wide_block(POS)] * 3 + [gg_spec],
        compiler_params=WIDE,
        cost_estimate=cost(14 * LIVE * LIVE * FEAT, 8),
    )(*places, norm_gains, sq, sk, sv, dso)
    gains = jnp.concatenate([gains_s, gains_t], axis=0)
    gains = gains + flips(gains, "dp", (1,))[0]
    gains = add_flips(gains, "dp", 2, 4)
    gains = add_flips(gains, "seq", 8, 16)
    gains = add_flips(gains, "seq", 2, 4)
    gains, back = lax.optimization_barrier((gains, back))
    gains = gains + flips(gains, "seq", (1,))[0]
    o, dtq, dtk = finish(back, [0, 1, 2])
    return o, dsq, dsk, dsv, dtq, dtk, gains


def solution(mesh):
    big = P("dp", "seq", None, None)
    return jax.shard_map(
        per_device,
        mesh=mesh,
        in_specs=(big,) * 6 + (P("dp", None), P("dp", None), P()),
        out_specs=(big,) * 6 + (P(),),
        check_vma=False,
    )
```
